32 devices in a mesh: leaf: 8 (over z, y), edge: 4 (over x, core).
Axes of the slice: x: 2, y: 2, z: 4, core: 2. Of those that a mesh axis runs over, the one named last changes fastest.
Arguments:
- positions: float32 [3, 139264], P(None, ('leaf', 'edge')), may hold values from -6 to 6
- density: bfloat16 [3, 139264], P(None, ('leaf', 'edge')), may hold values from -6 to 6
- self_operator: bfloat16 [1632, 1632], P('edge'), may hold values from -0.15625 to 0.15625
- owner: int32 [139264, 1], P(('leaf', 'edge')), may hold values from 0 to 7; in each aligned block of 4352 rows (0 to 4351, 4352 to 8703, ...) at most 816 rows name the same one
- near_tiles: int32 [1632, 3], P(('leaf', 'edge')), may hold values from 0 to 152, as said below
Outputs:
- velocity: float32 [3, 139264], P(None, ('leaf', 'edge'))
The draws below stay inside these ranges and needn't reach their ends.
Inputs may be any that keep to these rules, and one draw needn't show every extreme that they name: Among the rows of one device, at most 816 name the same owner; some owner reaches 816 in every draw. `near_tiles`: rows list leaves in the order of the points' blocks, 51 rows a leaf. Indices count the lower layer's 51 tiles, then the leaf's own, then the upper layer's. Column 0 names a tile of the lower layer, column 1 one of the upper layer, column 2 any tile.
All inputs are finite; a program needn't handle non-finite values.
Results may differ from the reference program's by a relative error of at most 0.00035.
Values may be sent and summed in bfloat16 or wider, within the bound.
A program may use at most 64 MiB of HBM per device.

```python
import math
import jax
import jax.numpy as jnp
import numpy as np
from jax import lax

NPT = 544
ORDER = 1632
PTS_DEV = 4352
NCELL = 256
NPTS = 139264
DEVICE_LEAF_SLOTS = 816
LEAF_SLOT_COUNT = 6528
TILES = 51
LEAF_TILES = 1632
N_LEAF = 8
N_EDGE = 4


def draw_near_tiles(key, part):
    row_count = LEAF_TILES
    first_key, second_key, third_key = jax.random.split(key, 3)
    lower_tile = jax.random.randint(first_key, (row_count, 1), 0, TILES)
    upper_tile = jax.random.randint(second_key, (row_count, 1), 2 * TILES, 3 * TILES)
    any_tile = jax.random.randint(third_key, (row_count, 1), 0, 3 * TILES)
    return jnp.concatenate([lower_tile, upper_tile, any_tile], axis=1).astype(jnp.int32)


def block_levels(key, dims, cuts, smallest, largest):
    loudness, own = 1.0, jax.random.fold_in(key, 6)
    for position, parts in cuts:
        heights = jnp.exp(jax.random.uniform(jax.random.fold_in(own, position), (parts,), jnp.float32, smallest / len(cuts), largest / len(cuts)))
        loudness = loudness * jnp.repeat(heights, dims[position] // parts).reshape([-1 if axis == position else 1 for axis in range(len(dims))])
    return loudness


def shared_out(own_key, own, number, rows, count, top, most, skew):
    sequence = jax.random.permutation(own_key, count)
    heavy_load, usual = load_shares(count, rows * top, most, skew, True), load_shares(count, rows * top, most, skew, False)
    places = jnp.arange(count)

    def named(tallies, turn):
        used = int((tallies > 0).sum())
        fixed = max(1, used // 4)
        passed = fixed + (places - fixed + turn * (used - fixed)) % max(1, count - fixed)
        return jnp.zeros((count,), jnp.int32).at[sequence[jnp.where(places < fixed, places, passed)]].set(jnp.asarray(tallies, jnp.int32))

    tallies = jnp.where(number % 4 == 0, named(heavy_load, number // 4), named(usual, number - number // 4 - 1))
    mixed = jax.random.permutation(jax.random.fold_in(own, 3), count)
    donor, receiver = mixed[0:count // 2 * 2:2], mixed[1:count // 2 * 2:2]
    slack = jnp.minimum(tallies[donor] - 1, most - tallies[receiver]) // 2
    slack = jnp.where((donor == sequence[0]) | (receiver == sequence[0]) | (tallies[receiver] == 0), 0, jnp.maximum(slack, 0))
    passed = jax.random.randint(jax.random.fold_in(own, 4), (count // 2,), 0, 1 << 20) % (slack + 1)
    tallies = tallies.at[donor].add(-passed).at[receiver].add(passed)
    members = jnp.searchsorted(jnp.cumsum(tallies), jnp.arange(rows * top), side="right").astype(jnp.int32)
    listing = members.reshape(top, rows).T
    listing = listing[jax.random.permutation(jax.random.fold_in(own, 1), rows)]
    turn = jax.random.randint(jax.random.fold_in(own, 2), (rows, 1), 0, top)
    return jnp.take_along_axis(listing, (jnp.arange(top)[None, :] + turn) % top, axis=1)


def load_shares(count, total, bound, skew, full):
    loads = [(1 << 20) // math.isqrt(standing ** skew) + 1 for standing in range(1, count + 1)]
    largest = bound if full else min(bound, max(-(-total // count), total * loads[0] // sum(loads)))
    least = 1 if total - largest >= count - 1 else 0
    given, rest = [largest] + [least] * (count - 1), total - largest - least * (count - 1)
    while rest > 0:
        candidates = [i for i in range(1, count) if given[i] < largest] or [i for i in range(1, count) if given[i] < bound]
        mass, left = sum([loads[i] for i in candidates]), rest
        for i in candidates:
            extra = min(bound - given[i], max(1, left * loads[i] // mass), rest)
            given[i] = given[i] + extra
            rest = rest - extra
    return np.array(given)


def noise(stream_key, extent, deviation, limit, pieces=(), kind=jnp.bfloat16):
    values = jax.random.normal(stream_key, extent, jnp.float32) * deviation
    if len(pieces) > 0:
        values = block_levels(stream_key, extent, pieces, -0.22, 0.18) * values
    return jnp.clip(values, min=-limit, max=limit).astype(kind)


def setup_inputs(seed: int = 0) -> dict:
    streams_of = jax.random.split(jax.random.key(seed), 6)
    positions = noise(streams_of[0], (3, NPTS), 1.0, 6.0, ((1, 32),), jnp.float32)
    density = noise(streams_of[1], (3, NPTS), 1.0, 6.0, ((1, 32),))
    self_operator = noise(streams_of[2], (ORDER, ORDER), ORDER ** -0.5, 0.15625, ((0, 4),))
    owner_keys = jax.random.split(jax.random.fold_in(streams_of[3], 1), NPTS // PTS_DEV)
    owner_turns = jax.random.permutation(jax.random.fold_in(streams_of[3], 3), NPTS // PTS_DEV)
    owner = jax.vmap(lambda own, number: shared_out(jax.random.fold_in(streams_of[3], 2), own, number, PTS_DEV, N_LEAF, 1, DEVICE_LEAF_SLOTS, 2))(owner_keys, owner_turns).reshape((NPTS, 1))
    near_tiles = draw_near_tiles(jax.random.fold_in(streams_of[5], 71), 0)
    return {"positions": positions, "density": density, "self_operator": self_operator, "owner": owner, "near_tiles": near_tiles}


reg_square = 0.05
kernel_scale = 1.0 / (8.0 * math.pi)

def tile_sum(pair_args):
    target, source = pair_args
    diff_x = target[0][:, None] - source[0][None, :]
    diff_y = target[1][:, None] - source[1][None, :]
    diff_z = target[2][:, None] - source[2][None, :]
    force_x = source[3][None, :]
    force_y = source[4][None, :]
    force_z = source[5][None, :]
    inverse = lax.rsqrt(diff_x * diff_x + diff_y * diff_y + diff_z * diff_z + reg_square)
    along = (diff_x * force_x + diff_y * force_y + diff_z * force_z) * inverse * inverse * inverse
    first = lax.optimization_barrier(jnp.sum(force_x * inverse + diff_x * along, axis=1))
    second = lax.optimization_barrier(jnp.sum(force_y * inverse + diff_y * along, axis=1))
    third = lax.optimization_barrier(jnp.sum(force_z * inverse + diff_z * along, axis=1))
    return jnp.stack([first, second, third], axis=0)

def stokeslet_sum(target_pos, source_block):
    result = lax.map(tile_sum, (target_pos.transpose(1, 0, 2), source_block.transpose(1, 0, 2)))
    return result.transpose(1, 0, 2)

def near_leaf(extended, tile_rows):
    home_tiles = extended[:, TILES:2 * TILES]
    summed = stokeslet_sum(home_tiles[0:3], home_tiles)
    for column in range(3):
        source_block = jnp.take(extended, tile_rows[:, column], axis=1)
        summed = summed + stokeslet_sum(home_tiles[0:3], source_block)
    return summed * kernel_scale

def point_ranks(owners):
    onehot = (owners[:, None] == jnp.arange(N_LEAF, dtype=jnp.int32)[None, :]).astype(jnp.int32)
    return lax.optimization_barrier(jnp.sum(jnp.cumsum(onehot, axis=0) * onehot, axis=1)) - 1

def reference(positions, density, self_operator, owner, near_tiles):
    block_groups = N_LEAF * N_EDGE
    cell_rows = density.reshape(3, NCELL, NPT).transpose(1, 0, 2).reshape(NCELL, ORDER)
    self_part = lax.dot_general(cell_rows, self_operator, (((1,), (1,)), ((), ())), preferred_element_type=jnp.float32)
    self_velocity = self_part.reshape(NCELL, 3, NPT).transpose(1, 0, 2).reshape(3, NPTS)
    blocks_by_owner = owner[:, 0].reshape(block_groups, PTS_DEV)
    slot_owner_rank = lax.map(point_ranks, blocks_by_owner)
    block_ids = jnp.arange(block_groups, dtype=jnp.int32)[:, None]
    source_octree_leaf = block_ids // N_EDGE
    octree_layer = block_ids % N_EDGE
    global_slot_index = ((blocks_by_owner * N_EDGE + octree_layer) * LEAF_SLOT_COUNT + source_octree_leaf * DEVICE_LEAF_SLOTS + slot_owner_rank).reshape(-1).astype(jnp.int32)
    message_content = jnp.concatenate([positions, density.astype(jnp.float32)], axis=0)
    points_per_leaf = jnp.zeros((6, block_groups * LEAF_SLOT_COUNT), jnp.float32).at[:, global_slot_index].set(message_content)
    points_per_leaf = points_per_leaf.reshape(6, block_groups, TILES, 128).transpose(1, 0, 2, 3)
    zero_leaf = jnp.zeros((1, 6, TILES, 128), jnp.float32)
    layers = jnp.arange(block_groups, dtype=jnp.int32) % N_EDGE
    lower_side = jnp.concatenate([zero_leaf, points_per_leaf[:-1]], axis=0)
    lower_side = jnp.where((layers > 0)[:, None, None, None], lower_side, 0.0)
    upper_side = jnp.concatenate([points_per_leaf[1:], zero_leaf], axis=0)
    upper_side = jnp.where((layers < N_EDGE - 1)[:, None, None, None], upper_side, 0.0)
    extended = jnp.concatenate([lower_side, points_per_leaf, upper_side], axis=2)
    tile_lists = near_tiles.reshape(block_groups, TILES, 3)
    near_field = lax.map(lambda pair_args: near_leaf(pair_args[0], pair_args[1]), (extended, tile_lists))
    flattened_near_field = near_field.transpose(1, 0, 2, 3).reshape(3, block_groups * LEAF_SLOT_COUNT)
    return self_velocity + jnp.take(flattened_near_field, global_slot_index, axis=1)
```

```python
import functools
import math

import jax
import jax.numpy as jnp
from jax import lax
from jax.experimental import pallas as pl
from jax.experimental.pallas import tpu as pltpu
from jax.sharding import PartitionSpec as P

NPT = 544
LANES = 128
GROUPS = 4
CUTS = (33, 46)

reg_square = 0.05
kernel_scale = 1.0 / (8.0 * math.pi)
NT = (((1,), (1,)), ((), ()))
TN = (((0,), (0,)), ((), ()))


def split3(x):
    hi = x.astype(jnp.bfloat16).astype(jnp.float32)
    rest = x - hi
    mid = rest.astype(jnp.bfloat16).astype(jnp.float32)
    return hi, mid, rest - mid


def split2(x):
    hi = x.astype(jnp.bfloat16)
    return hi, (x - hi.astype(jnp.float32)).astype(jnp.bfloat16)


def onehots(leafs, offset, own_ref, row_ref, lane_ref):
    points = own_ref.shape[1]
    win = row_ref.shape[0] // leafs
    chunks = points // LANES
    own = own_ref[...]
    ids = lax.broadcasted_iota(jnp.int32, (leafs, LANES), 0)
    hot = [jnp.where(own[:, c * LANES : (c + 1) * LANES] == ids, 1.0, 0.0) for c in range(chunks)]
    stacked = jnp.concatenate(hot, axis=0).astype(jnp.bfloat16)
    before = lax.broadcasted_iota(jnp.int32, (LANES, 2 * LANES), 0)
    after = lax.broadcasted_iota(jnp.int32, (LANES, 2 * LANES), 1)
    prefix = jnp.where((before < after), 1.0, 0.0).astype(jnp.bfloat16)
    counts = jnp.dot(stacked, prefix, preferred_element_type=jnp.float32)
    carry = jnp.zeros((leafs, LANES), jnp.float32) + offset.astype(jnp.float32)
    row_ids = lax.broadcasted_iota(jnp.int32, (leafs * win, LANES), 0)
    lane_ids = lax.broadcasted_iota(jnp.int32, (LANES, LANES), 0)
    for c in range(chunks):
        block = slice(c * leafs, (c + 1) * leafs)
        here = slice(c * LANES, (c + 1) * LANES)
        place = hot[c] * (counts[block, :LANES] + carry)
        carry = carry + counts[block, LANES:]
        slot = jnp.sum(place, axis=0, keepdims=True).astype(jnp.int32)
        row = own[:, here] * win + (slot >> 7)
        row_ref[:, here] = jnp.where(row == row_ids, 1.0, 0.0).astype(jnp.bfloat16)
        lane_ref[:, here] = jnp.where((slot & 127) == lane_ids, 1.0, 0.0).astype(jnp.bfloat16)


def scatter(leafs, pos_ref, den_ref, row_ref, lane_ref, spread_ref, send_ref):
    rows = row_ref.shape[0]
    win = rows // leafs
    pos = pos_ref[...]
    den = den_ref[...].astype(jnp.float32)
    parts = split3(pos)
    for k in range(12):
        part = den if k >= 9 else parts[k % 3]
        comp = k - 9 if k >= 9 else k // 3
        line = jnp.broadcast_to(part[comp : comp + 1], (16, pos.shape[1])).astype(jnp.bfloat16)
        for r in range(0, rows, 16):
            spread_ref[k * rows + r : k * rows + r + 16, :] = row_ref[r : r + 16, :] * line
    for begin, end in ((0, 6), (6, 12)):
        placed = lax.dot_general(
            spread_ref[begin * rows : end * rows, :], lane_ref[...], NT, preferred_element_type=jnp.float32
        )
        parts = [placed[r : r + rows] for r in range(0, (end - begin) * rows, rows)]
        if begin < 9:
            totals = [parts[r] + parts[r + 1] + parts[r + 2] for r in range(0, min(end, 9) - begin, 3)]
            totals += parts[9 - begin :]
        else:
            totals = parts
        for k, total in enumerate(totals):
            comp = begin // 3 + k
            for o in range(leafs):
                send_ref[o, comp] = total[o * win : (o + 1) * win]


def assemble(starts, recv_ref, tiles_ref):
    tiles_ref[...] = jnp.zeros_like(tiles_ref)
    win = recv_ref.shape[2]
    for l, start in enumerate(starts):
        for comp in range(6):
            tiles_ref[start : start + win, comp, :] += recv_ref[l, comp]


def features(tile, weight_ref, value_ref, target_ref):
    row = lax.broadcasted_iota(jnp.int32, (8, LANES), 0)
    first, last = row < 3, row == 7
    one = jnp.where(row == 6, 1.0, 0.0)
    pos = jnp.where(first, tile, 0.0)
    force = jnp.where(first, pltpu.roll(tile, 5, 0), 0.0)
    twice = force + jnp.where(first, 0.0, tile)
    hi, mid, low = split3(pos)
    hi_next, mid_next, low_next = (pltpu.roll(part, 3, 0) for part in (hi, mid, low))
    square = jnp.sum(pos * pos, axis=0, keepdims=True)
    along = jnp.sum(pos * force, axis=0, keepdims=True)
    zero = jnp.zeros_like(pos)
    pairs = (hi + hi_next, hi + mid_next, mid + low_next)
    r2_rows = [jnp.where(last, q, one - 2.0 * pair) for q, pair in zip(split3(square), pairs)]
    df_rows = [jnp.where(last, q, f) for q, f in zip(split3(-along), (twice, force, zero))]
    weight_ref[...] = jnp.concatenate(
        [jnp.concatenate(r2_rows + [zero], axis=0), jnp.concatenate(df_rows + [zero], axis=0)], axis=1
    ).astype(jnp.bfloat16)
    if target_ref is not None:
        pairs = (hi + mid_next, low + hi_next, mid + hi_next)
        fixed = jnp.where(last, 1.0, 0.0)
        rows = [fixed + pair + one * q for q, pair in zip(split3(square + reg_square), pairs)]
        target_ref[...] = jnp.concatenate(rows + [zero], axis=0).astype(jnp.bfloat16)
    a_low = one - hi
    value = jnp.concatenate([force, force, a_low - mid_next, a_low], axis=1)
    value_ref[...] = jnp.concatenate([value, jnp.zeros_like(value)], axis=0).astype(jnp.bfloat16)


def near_tile(tile, target, sources):
    blocks, values = [], []
    for weight, value in sources:
        both = lax.dot_general(weight, target, TN, preferred_element_type=jnp.float32)
        inverse = lax.rsqrt(both[:LANES])
        along = both[LANES:] * inverse * (inverse * inverse)
        blocks.extend(split2(inverse) + split2(along))
        values.append(value)
    sums = jnp.dot(
        jnp.concatenate(values, axis=1), jnp.concatenate(blocks, axis=0),
        preferred_element_type=jnp.float32,
    )[:8]
    row = lax.broadcasted_iota(jnp.int32, (8, LANES), 0)
    pos = jnp.where(row < 3, tile, 0.0)
    return (sums + pltpu.roll(sums, 5, 0) + pos * sums[6:7]) * kernel_scale


def pair_sums(target, sources):
    weights = jnp.concatenate([weight for weight, _ in sources], axis=1)
    both = lax.dot_general(target, weights, TN, preferred_element_type=jnp.float32)
    blocks = []
    for s in range(len(sources)):
        first = 2 * LANES * s
        inverse = lax.rsqrt(both[:, first : first + LANES])
        along = both[:, first + LANES : first + 2 * LANES] * inverse * (inverse * inverse)
        blocks.extend(split2(inverse) + split2(along))
    return lax.dot_general(
        jnp.concatenate([value for _, value in sources], axis=1), jnp.concatenate(blocks, axis=1), NT,
        preferred_element_type=jnp.float32,
    )[:8]


def list_steps(begin, end, origin, tiles, lists_ref, tiles_ref, weight_ref, value_ref, target_ref, near_ref):
    row = lax.broadcasted_iota(jnp.int32, (8, LANES), 0)

    def step(i, carry):
        j = lax.rem(origin + i, tiles)
        indices = [tiles + j] + [lists_ref[column, j] for column in range(3)]
        sums = pair_sums(target_ref[j], [(weight_ref[s], value_ref[s]) for s in indices])
        pos = jnp.where(row < 3, tiles_ref[1, j], 0.0)
        near_ref[j] = (sums + pltpu.roll(sums, 5, 0) + pos * sums[6:7]) * kernel_scale
        return carry

    lax.fori_loop(begin, end, step, 0, unroll=end - begin)


def gather(leafs, get_near, row_ref, lane_ref, self_ref, out_ref):
    rows = row_ref.shape[0]
    points = out_ref.shape[1]
    split = []
    for comp in range(3):
        block = jnp.concatenate([get_near(o, comp) for o in range(leafs)], axis=0)
        split.append(jnp.concatenate(split2(block), axis=1))
    near = jnp.concatenate(split, axis=0)
    for begin in range(0, points, 2 * LANES):
        here = slice(begin, begin + 2 * LANES)
        lane = lane_ref[:, here]
        found = jnp.dot(
            near, jnp.concatenate([lane, lane], axis=0), preferred_element_type=jnp.float32
        )
        row = row_ref[:, here].astype(jnp.float32)
        for comp in range(3):
            picked = found[comp * rows : (comp + 1) * rows] * row
            out_ref[comp : comp + 1, here] = (
                jnp.sum(picked, axis=0, keepdims=True) + self_ref[comp : comp + 1, here]
            )


def pre_kernel(leafs, slots, own_ref, pos_ref, den_ref, send_ref, row_ref, lane_ref, spread_ref):
    offset = lax.rem(lax.axis_index("leaf") * slots, LANES)
    onehots(leafs, offset, own_ref, row_ref, lane_ref)
    scatter(leafs, pos_ref, den_ref, row_ref, lane_ref, spread_ref, send_ref)


def build_layer(tiles, starts, layer, recv, tiles_ref, weight_ref, value_ref, target_ref):
    assemble(starts, recv, tiles_ref.at[layer])

    def build(j, carry):
        index = layer * tiles + j
        features(tiles_ref[layer, j], weight_ref.at[index], value_ref.at[index],
                 target_ref.at[j] if layer == 1 else None)
        return carry

    lax.fori_loop(0, tiles, build, 0, unroll=3)


def near_steps(begin, end, tiles, lists_ref, tiles_ref, weight_ref, value_ref, target_ref, near_ref, unroll):
    def step(j, carry):
        indices = [tiles + j] + [lists_ref[column, j] for column in range(3)]
        near_ref[j] = near_tile(tiles_ref[1, j], target_ref[j],
                                [(weight_ref[i], value_ref[i]) for i in indices])
        return carry

    lax.fori_loop(begin, end, step, 0, unroll=unroll)


def near_kernel(tiles, starts, lists_ref, own_ref, low_ref, high_ref, ret_ref, tiles_ref, *matrices):
    *features_refs, near_ref = matrices
    for layer, recv in enumerate((low_ref, own_ref, high_ref)):
        build_layer(tiles, starts, layer, recv, tiles_ref, *features_refs)
    near_ref[...] = jnp.zeros_like(near_ref)
    near_steps(0, tiles, tiles, lists_ref, tiles_ref, *matrices, 3)
    for l, start in enumerate(starts):
        for comp in range(3):
            ret_ref[l, comp] = near_ref[start : start + ret_ref.shape[2], comp, :]


def post_kernel(leafs, back_ref, row_ref, lane_ref, self_ref, out_ref):
    gather(leafs, lambda o, comp: back_ref[o, comp], row_ref, lane_ref, self_ref, out_ref)


def fused_kernel(leafs, edges, slots, tiles, starts, lists_hbm, own_hbm, pos_hbm, den_hbm, operator_hbm,
                 out_ref, lists_ref, own_ref, pos_ref, den_ref, operator_ref, cells_ref, wide_ref, row_ref, lane_ref, spread_ref, send_ref, windows_ref,
                 tiles_ref, weight_ref, value_ref, target_ref, near_ref, ret_ref, back_ref,
                 group_ref, partial_ref, parts_ref, whole_ref, self_ref,
                 load_sems, cell_sems, part_sems, point_sems, edge_sems, back_sems):
    loads = [pltpu.make_async_copy(own_hbm, own_ref, load_sems.at[0]),
             pltpu.make_async_copy(pos_hbm, pos_ref, load_sems.at[1]),
             pltpu.make_async_copy(den_hbm, den_ref, load_sems.at[2]),
             pltpu.make_async_copy(lists_hbm, lists_ref, load_sems.at[3]),
             pltpu.make_async_copy(operator_hbm, operator_ref, load_sems.at[4])]
    for load in loads:
        load.start()
    leaf, edge = lax.axis_index("leaf"), lax.axis_index("edge")
    barrier = pltpu.get_barrier_semaphore()
    for d in range(1, leafs):
        pl.semaphore_signal(barrier, inc=1, device_id={"leaf": lax.rem(leaf + d, leafs)})
    for d in range(1, edges):
        pl.semaphore_signal(barrier, inc=1, device_id={"edge": lax.rem(edge + d, edges)})

    def remote(src, dst, sems, index, **device):
        return pltpu.make_async_remote_copy(
            src_ref=src, dst_ref=dst, send_sem=sems.at[0, index], recv_sem=sems.at[1, index],
            device_id=device,
        )

    loads[0].wait()
    onehots(leafs, lax.rem(leaf * slots, LANES), own_ref, row_ref, lane_ref)
    loads[1].wait()
    loads[2].wait()
    scatter(leafs, pos_ref, den_ref, row_ref, lane_ref, spread_ref, send_ref)
    pl.semaphore_wait(barrier, leafs + edges - 2)

    points = []
    for d in range(1, leafs):
        to = lax.rem(leaf + d, leafs)
        points.append(remote(send_ref.at[to], windows_ref.at[1, leaf], point_sems, d, leaf=to))
        points[-1].start()
    count = parts_ref.shape[1]
    wide_ref[...] = jnp.zeros_like(wide_ref)
    dense = den_ref[...].astype(jnp.float32)
    for c in range(count):
        for k in range(3):
            wide_ref[c : c + 1, k * NPT : (k + 1) * NPT] = dense[k : k + 1, c * NPT : (c + 1) * NPT]
    cells_ref[...] = wide_ref[...].astype(jnp.bfloat16)
    cells = []
    for d in range(1, edges):
        to = lax.rem(edge + d, edges)
        cells.append(remote(cells_ref, group_ref.at[edge], cell_sems, d, edge=to))
        cells[-1].start()
    windows_ref[1, leaf] = send_ref[leaf]
    group_ref[edge] = cells_ref[...]

    has_up, has_down = edge < edges - 1, edge > 0

    def forward(source, d):
        up = remote(windows_ref.at[1, source], windows_ref.at[0, source], edge_sems.at[0], d,
                    edge=jnp.minimum(edge + 1, edges - 1))
        down = remote(windows_ref.at[1, source], windows_ref.at[2, source], edge_sems.at[1], d,
                      edge=jnp.maximum(edge - 1, 0))
        return up, down

    def start_forward(source, d):
        up, down = forward(source, d)
        pl.when(has_up)(up.start)
        pl.when(has_down)(down.start)

    start_forward(leaf, 0)
    for copy in cells:
        copy.wait()
    loads[4].wait()
    group = group_ref[...].reshape(edges * group_ref.shape[1], group_ref.shape[2])
    partial = lax.dot_general(group, operator_ref[...], NT, preferred_element_type=jnp.float32)
    partial_ref[...] = partial.reshape(partial_ref.shape)
    parts = []
    for d in range(1, edges):
        to = lax.rem(edge + d, edges)
        parts.append(remote(partial_ref.at[to, pl.ds(0, count)], parts_ref.at[edge], part_sems, d, edge=to))
        parts[-1].start()
    parts_ref[edge] = partial_ref[edge, pl.ds(0, count)]

    for d in range(1, leafs):
        points[d - 1].wait()
        start_forward(lax.rem(leaf + leafs - d, leafs), d)

    @pl.when(edge == 0)
    def _():
        windows_ref[0] = jnp.zeros_like(windows_ref[0])

    @pl.when(edge == edges - 1)
    def _():
        windows_ref[2] = jnp.zeros_like(windows_ref[2])

    matrices = (weight_ref, value_ref, target_ref)
    build_layer(tiles, starts, 1, windows_ref.at[1], tiles_ref, *matrices)
    near_ref[tiles:] = jnp.zeros_like(near_ref[tiles:])
    flights = [forward(lax.rem(leaf + leafs - d, leafs), d) for d in range(leafs)]
    for up, down in flights:
        pl.when(has_down)(up.wait_recv)
    build_layer(tiles, starts, 0, windows_ref.at[0], tiles_ref, *matrices)
    for up, down in flights:
        pl.when(has_up)(down.wait_recv)
        pl.when(has_up)(up.wait_send)
        pl.when(has_down)(down.wait_send)
    build_layer(tiles, starts, 2, windows_ref.at[2], tiles_ref, *matrices)

    win = ret_ref.shape[2]
    back = [remote(ret_ref.at[d], back_ref.at[leaf], back_sems, d, leaf=lax.rem(leaf + d, leafs))
            for d in range(1, leafs)]
    loads[3].wait()
    origin = (leaf + 1) * slots // LANES
    done, sent = 0, 1
    for end in [cut for cut in CUTS if cut < tiles] + [tiles]:
        list_steps(done, end, origin, tiles, lists_ref, tiles_ref, *matrices, near_ref)
        done = end
        while sent < leafs and (sent * slots + LANES - 1) // LANES + 1 <= done:
            to = lax.rem(leaf + sent, leafs)
            first = to * slots // LANES
            for comp in range(3):
                ret_ref[sent, comp] = near_ref[pl.ds(first, win), comp, :]
            back[sent - 1].start()
            sent += 1
    first = leaf * slots // LANES
    for comp in range(3):
        back_ref[leaf, comp] = near_ref[pl.ds(first, win), comp, :]
    for copy in parts:
        copy.wait()
    share = parts_ref.shape[2]
    for e in range(edges):
        whole_ref[:, e * share : (e + 1) * share] = parts_ref[e]
    for c in range(count):
        for k in range(3):
            self_ref[k : k + 1, c * NPT : (c + 1) * NPT] = whole_ref[c : c + 1, k * NPT : (k + 1) * NPT]
    for copy in back:
        copy.wait()
    gather(leafs, lambda o, comp: back_ref[o, comp], row_ref, lane_ref, self_ref, out_ref)


VM = pl.BlockSpec(memory_space=pltpu.VMEM)
PARAMS = pltpu.CompilerParams(vmem_limit_bytes=48 * 2**20)


def self_part(density):
    cell_count = density.shape[1] // NPT
    return density.reshape(3, cell_count, NPT).transpose(1, 0, 2).reshape(cell_count, 3 * NPT)


def fast(positions, density, self_operator, owner, near_tiles):
    points = density.shape[1]
    cell_count = points // NPT
    leafs = lax.axis_size("leaf")
    slots = 3 * points // (2 * leafs)
    tiles = slots * leafs // LANES
    starts = [l * slots // LANES for l in range(leafs)]
    win = max((l * slots % LANES + slots - 1) // LANES + 1 for l in range(leafs))
    padded_tiles = -(-max(tiles, starts[-1] + win) // 8) * 8
    rows = leafs * win
    f32, bf16 = jnp.float32, jnp.bfloat16
    shape = jax.ShapeDtypeStruct

    edges = lax.axis_size("edge")
    matrices = [
        pltpu.VMEM((3, padded_tiles, 8, LANES), f32),
        pltpu.VMEM((3 * tiles, 8 * GROUPS, 2 * LANES), bf16),
        pltpu.VMEM((3 * tiles, 16, 4 * LANES), bf16),
        pltpu.VMEM((tiles, 8 * GROUPS, LANES), bf16),
        pltpu.VMEM((padded_tiles, 8, LANES), f32),
    ]
    if leafs <= 8:
        group = -(-cell_count // 16) * 16
        sems = pltpu.SemaphoreType.DMA
        return pl.pallas_call(
            functools.partial(fused_kernel, leafs, edges, slots, tiles, starts),
            out_shape=shape((3, points), f32),
            in_specs=[pl.BlockSpec(memory_space=pltpu.HBM)] * 5,
            out_specs=VM,
            scratch_shapes=[
                pltpu.SMEM((3, tiles), jnp.int32),
                pltpu.VMEM((1, points), jnp.int32),
                pltpu.VMEM((3, points), f32),
                pltpu.VMEM((3, points), bf16),
                pltpu.VMEM(self_operator.shape, bf16),
                pltpu.VMEM((group, 3 * NPT), bf16),
                pltpu.VMEM((group, 3 * NPT), f32),
                pltpu.VMEM((rows, points), bf16),
                pltpu.VMEM((LANES, points), bf16),
                pltpu.VMEM((12 * rows, points), bf16),
                pltpu.VMEM((leafs, 6, win, LANES), f32),
                pltpu.VMEM((3, leafs, 6, win, LANES), f32),
                *matrices,
                pltpu.VMEM((leafs, 3, win, LANES), f32),
                pltpu.VMEM((leafs, 3, win, LANES), f32),
                pltpu.VMEM((edges, group, 3 * NPT), bf16),
                pltpu.VMEM((edges, group, self_operator.shape[0]), f32),
                pltpu.VMEM((edges, cell_count, self_operator.shape[0]), f32),
                pltpu.VMEM((cell_count, 3 * NPT), f32),
                pltpu.VMEM((3, points), f32),
                sems((5,)), sems((2, edges)), sems((2, edges)), sems((2, leafs)), sems((2, 2, leafs)),
                sems((2, leafs)),
            ],
            compiler_params=pltpu.CompilerParams(
                vmem_limit_bytes=62 * 2**20, collective_id=0, has_side_effects=True
            ),
            name="fused",
        )(near_tiles.T, owner.reshape(1, points), positions, density, self_operator)

    send, row_hot, lane_hot = pl.pallas_call(
        functools.partial(pre_kernel, leafs, slots),
        out_shape=(shape((leafs, 6, win, LANES), f32), shape((rows, points), bf16),
                   shape((LANES, points), bf16)),
        in_specs=[VM] * 3, out_specs=(VM,) * 3,
        scratch_shapes=[pltpu.VMEM((12 * rows, points), bf16)],
        compiler_params=PARAMS, name="pre",
    )(owner.reshape(1, points), positions, density)
    received = lax.all_to_all(send, "leaf", split_axis=0, concat_axis=0, tiled=True)
    up = [(i, i + 1) for i in range(edges - 1)]
    low = lax.ppermute(received, "edge", up)
    high = lax.ppermute(received, "edge", [(b, a) for a, b in up])

    group_rows = lax.all_gather(self_part(density), "edge", axis=0, tiled=True)
    partial_rows = lax.dot_general(group_rows, self_operator, NT, preferred_element_type=f32)
    rows_back = lax.all_to_all(partial_rows, "edge", split_axis=0, concat_axis=1, tiled=True)
    self_velocity = rows_back.reshape(cell_count, 3, NPT).transpose(1, 0, 2).reshape(3, points)

    result = pl.pallas_call(
        functools.partial(near_kernel, tiles, starts),
        out_shape=shape((leafs, 3, win, LANES), f32),
        in_specs=[pl.BlockSpec(memory_space=pltpu.SMEM), VM, VM, VM], out_specs=VM,
        scratch_shapes=matrices,
        compiler_params=PARAMS, name="near",
    )(near_tiles.T, received, low, high)
    back = lax.all_to_all(result, "leaf", split_axis=0, concat_axis=0, tiled=True)
    return pl.pallas_call(
        functools.partial(post_kernel, leafs),
        out_shape=shape((3, points), f32),
        in_specs=[VM] * 4, out_specs=VM, compiler_params=PARAMS, name="post",
    )(back, row_hot, lane_hot, self_velocity)


def solution(mesh):
    placed = (
        P(None, ("leaf", "edge")),
        P(None, ("leaf", "edge")),
        P("edge", None),
        P(("leaf", "edge"), None),
        P(("leaf", "edge"), None),
    )
    return jax.shard_map(
        fast, mesh=mesh, in_specs=placed, out_specs=P(None, ("leaf", "edge")), check_vma=False
    )
```

```python
import functools
import math

import jax
import jax.numpy as jnp
from jax import lax
from jax.experimental import pallas as pl
from jax.experimental.pallas import tpu as pltpu
from jax.sharding import PartitionSpec as P

NPT = 544
LANES = 128
GROUPS = 4
CUTS = (33, 46)

reg_square = 0.05
kernel_scale = 1.0 / (8.0 * math.pi)
NT = (((1,), (1,)), ((), ()))
TN = (((0,), (0,)), ((), ()))


def split3(x):
    hi = x.astype(jnp.bfloat16).astype(jnp.float32)
    rest = x - hi
    mid = rest.astype(jnp.bfloat16).astype(jnp.float32)
    return hi, mid, rest - mid


def split2(x):
    hi = x.astype(jnp.bfloat16)
    return hi, (x - hi.astype(jnp.float32)).astype(jnp.bfloat16)


def onehots(leafs, offset, own_ref, row_ref, lane_ref):
    points = own_ref.shape[1]
    win = row_ref.shape[0] // leafs
    chunks = points // LANES
    own = own_ref[...]
    ids = lax.broadcasted_iota(jnp.int32, (leafs, LANES), 0)
    hot = [jnp.where(own[:, c * LANES : (c + 1) * LANES] == ids, 1.0, 0.0) for c in range(chunks)]
    stacked = jnp.concatenate(hot, axis=0).astype(jnp.bfloat16)
    before = lax.broadcasted_iota(jnp.int32, (LANES, 2 * LANES), 0)
    after = lax.broadcasted_iota(jnp.int32, (LANES, 2 * LANES), 1)
    prefix = jnp.where((before < after), 1.0, 0.0).astype(jnp.bfloat16)
    counts = jnp.dot(stacked, prefix, preferred_element_type=jnp.float32)
    carry = jnp.zeros((leafs, LANES), jnp.float32) + offset.astype(jnp.float32)
    row_ids = lax.broadcasted_iota(jnp.int32, (leafs * win, LANES), 0)
    lane_ids = lax.broadcasted_iota(jnp.int32, (LANES, LANES), 0)
    for c in range(chunks):
        block = slice(c * leafs, (c + 1) * leafs)
        here = slice(c * LANES, (c + 1) * LANES)
        place = hot[c] * (counts[block, :LANES] + carry)
        carry = carry + counts[block, LANES:]
        slot = jnp.sum(place, axis=0, keepdims=True).astype(jnp.int32)
        row = own[:, here] * win + (slot >> 7)
        row_ref[:, here] = jnp.where(row == row_ids, 1.0, 0.0).astype(jnp.bfloat16)
        lane_ref[:, here] = jnp.where((slot & 127) == lane_ids, 1.0, 0.0).astype(jnp.bfloat16)


def scatter(leafs, pos_ref, den_ref, row_ref, lane_ref, spread_ref, send_ref):
    rows = row_ref.shape[0]
    win = rows // leafs
    pos = pos_ref[...]
    den = den_ref[...].astype(jnp.float32)
    parts = split3(pos)
    for k in range(12):
        part = den if k >= 9 else parts[k % 3]
        comp = k - 9 if k >= 9 else k // 3
        line = jnp.broadcast_to(part[comp : comp + 1], (16, pos.shape[1])).astype(jnp.bfloat16)
        for r in range(0, rows, 16):
            spread_ref[k * rows + r : k * rows + r + 16, :] = row_ref[r : r + 16, :] * line
    for begin, end in ((0, 6), (6, 12)):
        placed = lax.dot_general(
            spread_ref[begin * rows : end * rows, :], lane_ref[...], NT, preferred_element_type=jnp.float32
        )
        parts = [placed[r : r + rows] for r in range(0, (end - begin) * rows, rows)]
        if begin < 9:
            totals = [parts[r] + parts[r + 1] + parts[r + 2] for r in range(0, min(end, 9) - begin, 3)]
            totals += parts[9 - begin :]
        else:
            totals = parts
        for k, total in enumerate(totals):
            comp = begin // 3 + k
            for o in range(leafs):
                send_ref[o, comp] = total[o * win : (o + 1) * win]


def scatter_halves(leafs, pos_ref, den_ref, row_ref, lane_ref, spread_ref, send_ref):
    rows = row_ref.shape[0]
    win = rows // leafs
    pos = pos_ref[...]
    den = den_ref[...].astype(jnp.float32)
    high = pos.astype(jnp.bfloat16).astype(jnp.float32)
    parts = (high, pos - high)
    for k in range(9):
        part, comp = (parts[k % 2], k // 2) if k < 6 else (den, k - 6)
        line = jnp.broadcast_to(part[comp : comp + 1], (16, pos.shape[1])).astype(jnp.bfloat16)
        for r in range(0, rows, 16):
            spread_ref[k * rows + r : k * rows + r + 16, :] = row_ref[r : r + 16, :] * line
    placed = []
    for begin, end in ((0, 5), (5, 9)):
        found = lax.dot_general(
            spread_ref[begin * rows : end * rows, :], lane_ref[...], NT, preferred_element_type=jnp.float32
        )
        placed += [found[k * rows : (k + 1) * rows] for k in range(end - begin)]
    empty = jnp.zeros((send_ref.shape[1] - 9 * win, LANES), jnp.float32)
    for o in range(leafs):
        here = [part[o * win : (o + 1) * win] for part in placed] + [empty]
        send_ref[o] = jnp.concatenate(here, axis=0).astype(jnp.bfloat16)


def assemble_halves(starts, win, recv_ref, tiles_ref):
    tiles_ref[...] = jnp.zeros_like(tiles_ref)
    for l, start in enumerate(starts):
        window = recv_ref[l].astype(jnp.float32)
        parts = [window[k * win : (k + 1) * win] for k in range(9)]
        comps = [parts[0] + parts[1], parts[2] + parts[3], parts[4] + parts[5]] + parts[6:]
        for comp in range(6):
            tiles_ref[start : start + win, comp, :] += comps[comp]


def assemble(starts, recv_ref, tiles_ref):
    tiles_ref[...] = jnp.zeros_like(tiles_ref)
    win = recv_ref.shape[2]
    for l, start in enumerate(starts):
        for comp in range(6):
            tiles_ref[start : start + win, comp, :] += recv_ref[l, comp]


def features(tile, weight_ref, value_ref, target_ref):
    row = lax.broadcasted_iota(jnp.int32, (8, LANES), 0)
    first, last = row < 3, row == 7
    one = jnp.where(row == 6, 1.0, 0.0)
    pos = jnp.where(first, tile, 0.0)
    force = jnp.where(first, pltpu.roll(tile, 5, 0), 0.0)
    twice = force + jnp.where(first, 0.0, tile)
    hi, mid, low = split3(pos)
    hi_next, mid_next, low_next = (pltpu.roll(part, 3, 0) for part in (hi, mid, low))
    square = jnp.sum(pos * pos, axis=0, keepdims=True)
    along = jnp.sum(pos * force, axis=0, keepdims=True)
    zero = jnp.zeros_like(pos)
    pairs = (hi + hi_next, hi + mid_next, mid + low_next)
    r2_rows = [jnp.where(last, q, one - 2.0 * pair) for q, pair in zip(split3(square), pairs)]
    df_rows = [jnp.where(last, q, f) for q, f in zip(split3(-along), (twice, force, zero))]
    weight_ref[...] = jnp.concatenate(
        [jnp.concatenate(r2_rows + [zero], axis=0), jnp.concatenate(df_rows + [zero], axis=0)], axis=1
    ).astype(jnp.bfloat16)
    if target_ref is not None:
        pairs = (hi + mid_next, low + hi_next, mid + hi_next)
        fixed = jnp.where(last, 1.0, 0.0)
        rows = [fixed + pair + one * q for q, pair in zip(split3(square + reg_square), pairs)]
        target_ref[...] = jnp.concatenate(rows + [zero], axis=0).astype(jnp.bfloat16)
    a_low = one - hi
    value = jnp.concatenate([force, force, a_low - mid_next, a_low], axis=1)
    value_ref[...] = jnp.concatenate([value, jnp.zeros_like(value)], axis=0).astype(jnp.bfloat16)


def near_tile(tile, target, sources):
    blocks, values = [], []
    for weight, value in sources:
        both = lax.dot_general(weight, target, TN, preferred_element_type=jnp.float32)
        inverse = lax.rsqrt(both[:LANES])
        along = both[LANES:] * inverse * (inverse * inverse)
        blocks.extend(split2(inverse) + split2(along))
        values.append(value)
    sums = jnp.dot(
        jnp.concatenate(values, axis=1), jnp.concatenate(blocks, axis=0),
        preferred_element_type=jnp.float32,
    )[:8]
    row = lax.broadcasted_iota(jnp.int32, (8, LANES), 0)
    pos = jnp.where(row < 3, tile, 0.0)
    return (sums + pltpu.roll(sums, 5, 0) + pos * sums[6:7]) * kernel_scale


def pair_sums(target, sources):
    weights = jnp.concatenate([weight for weight, _ in sources], axis=1)
    both = lax.dot_general(target, weights, TN, preferred_element_type=jnp.float32)
    blocks = []
    for s in range(len(sources)):
        first = 2 * LANES * s
        inverse = lax.rsqrt(both[:, first : first + LANES])
        along = both[:, first + LANES : first + 2 * LANES] * inverse * (inverse * inverse)
        blocks.extend(split2(inverse) + split2(along))
    return lax.dot_general(
        jnp.concatenate([value for _, value in sources], axis=1), jnp.concatenate(blocks, axis=1), NT,
        preferred_element_type=jnp.float32,
    )[:8]


def list_steps(begin, end, origin, tiles, lists_ref, tiles_ref, weight_ref, value_ref, target_ref, near_ref):
    row = lax.broadcasted_iota(jnp.int32, (8, LANES), 0)

    def step(i, carry):
        j = lax.rem(origin + i, tiles)
        indices = [tiles + j] + [lists_ref[column, j] for column in range(3)]
        sums = pair_sums(target_ref[j], [(weight_ref[s], value_ref[s]) for s in indices])
        pos = jnp.where(row < 3, tiles_ref[1, j], 0.0)
        near_ref[j] = (sums + pltpu.roll(sums, 5, 0) + pos * sums[6:7]) * kernel_scale
        return carry

    lax.fori_loop(begin, end, step, 0, unroll=end - begin)


def gather(leafs, get_near, row_ref, lane_ref, self_ref, out_ref):
    rows = row_ref.shape[0]
    points = out_ref.shape[1]
    split = []
    for comp in range(3):
        block = jnp.concatenate([get_near(o, comp) for o in range(leafs)], axis=0)
        split.append(jnp.concatenate(split2(block), axis=1))
    near = jnp.concatenate(split, axis=0)
    for begin in range(0, points, 2 * LANES):
        here = slice(begin, begin + 2 * LANES)
        lane = lane_ref[:, here]
        found = jnp.dot(
            near, jnp.concatenate([lane, lane], axis=0), preferred_element_type=jnp.float32
        )
        row = row_ref[:, here].astype(jnp.float32)
        for comp in range(3):
            picked = found[comp * rows : (comp + 1) * rows] * row
            out_ref[comp : comp + 1, here] = (
                jnp.sum(picked, axis=0, keepdims=True) + self_ref[comp : comp + 1, here]
            )


def pre_kernel(leafs, slots, own_ref, pos_ref, den_ref, send_ref, row_ref, lane_ref, spread_ref):
    offset = lax.rem(lax.axis_index("leaf") * slots, LANES)
    onehots(leafs, offset, own_ref, row_ref, lane_ref)
    scatter(leafs, pos_ref, den_ref, row_ref, lane_ref, spread_ref, send_ref)


def build_layer(tiles, starts, layer, recv, tiles_ref, weight_ref, value_ref, target_ref, win=None):
    if win is None:
        assemble(starts, recv, tiles_ref.at[layer])
    else:
        assemble_halves(starts, win, recv, tiles_ref.at[layer])

    def build(j, carry):
        index = layer * tiles + j
        features(tiles_ref[layer, j], weight_ref.at[index], value_ref.at[index],
                 target_ref.at[j] if layer == 1 else None)
        return carry

    lax.fori_loop(0, tiles, build, 0, unroll=3)


def near_steps(begin, end, tiles, lists_ref, tiles_ref, weight_ref, value_ref, target_ref, near_ref, unroll):
    def step(j, carry):
        indices = [tiles + j] + [lists_ref[column, j] for column in range(3)]
        near_ref[j] = near_tile(tiles_ref[1, j], target_ref[j],
                                [(weight_ref[i], value_ref[i]) for i in indices])
        return carry

    lax.fori_loop(begin, end, step, 0, unroll=unroll)


def near_kernel(tiles, starts, lists_ref, own_ref, low_ref, high_ref, ret_ref, tiles_ref, *matrices):
    *features_refs, near_ref = matrices
    for layer, recv in enumerate((low_ref, own_ref, high_ref)):
        build_layer(tiles, starts, layer, recv, tiles_ref, *features_refs)
    near_ref[...] = jnp.zeros_like(near_ref)
    near_steps(0, tiles, tiles, lists_ref, tiles_ref, *matrices, 3)
    for l, start in enumerate(starts):
        for comp in range(3):
            ret_ref[l, comp] = near_ref[start : start + ret_ref.shape[2], comp, :]


def post_kernel(leafs, back_ref, row_ref, lane_ref, self_ref, out_ref):
    gather(leafs, lambda o, comp: back_ref[o, comp], row_ref, lane_ref, self_ref, out_ref)


def fused_kernel(leafs, edges, slots, tiles, starts, lists_hbm, own_hbm, pos_hbm, den_hbm, operator_hbm,
                 out_ref, lists_ref, own_ref, pos_ref, den_ref, operator_ref, cells_ref, wide_ref, row_ref, lane_ref, spread_ref, send_ref, windows_ref,
                 tiles_ref, weight_ref, value_ref, target_ref, near_ref, ret_ref, back_ref,
                 group_ref, partial_ref, parts_ref, whole_ref, self_ref,
                 load_sems, cell_sems, part_sems, point_sems, edge_sems, back_sems):
    loads = [pltpu.make_async_copy(own_hbm, own_ref, load_sems.at[0]),
             pltpu.make_async_copy(pos_hbm, pos_ref, load_sems.at[1]),
             pltpu.make_async_copy(den_hbm, den_ref, load_sems.at[2]),
             pltpu.make_async_copy(lists_hbm, lists_ref, load_sems.at[3]),
             pltpu.make_async_copy(operator_hbm, operator_ref, load_sems.at[4])]
    for load in loads:
        load.start()
    win = ret_ref.shape[2]
    leaf, edge = lax.axis_index("leaf"), lax.axis_index("edge")
    barrier = pltpu.get_barrier_semaphore()
    for d in range(1, leafs):
        pl.semaphore_signal(barrier, inc=1, device_id={"leaf": lax.rem(leaf + d, leafs)})
    for d in range(1, edges):
        pl.semaphore_signal(barrier, inc=1, device_id={"edge": lax.rem(edge + d, edges)})

    def remote(src, dst, sems, index, **device):
        return pltpu.make_async_remote_copy(
            src_ref=src, dst_ref=dst, send_sem=sems.at[0, index], recv_sem=sems.at[1, index],
            device_id=device,
        )

    loads[0].wait()
    onehots(leafs, lax.rem(leaf * slots, LANES), own_ref, row_ref, lane_ref)
    loads[1].wait()
    loads[2].wait()
    scatter_halves(leafs, pos_ref, den_ref, row_ref, lane_ref, spread_ref, send_ref)
    pl.semaphore_wait(barrier, leafs + edges - 2)

    points = []
    for d in range(1, leafs):
        to = lax.rem(leaf + d, leafs)
        points.append(remote(send_ref.at[to], windows_ref.at[1, leaf], point_sems, d, leaf=to))
        points[-1].start()
    count = parts_ref.shape[1]
    wide_ref[...] = jnp.zeros_like(wide_ref)
    dense = den_ref[...].astype(jnp.float32)
    for c in range(count):
        for k in range(3):
            wide_ref[c : c + 1, k * NPT : (k + 1) * NPT] = dense[k : k + 1, c * NPT : (c + 1) * NPT]
    cells_ref[...] = wide_ref[...].astype(jnp.bfloat16)
    cells = []
    for d in range(1, edges):
        to = lax.rem(edge + d, edges)
        cells.append(remote(cells_ref, group_ref.at[edge], cell_sems, d, edge=to))
        cells[-1].start()
    windows_ref[1, leaf] = send_ref[leaf]
    group_ref[edge] = cells_ref[...]

    has_up, has_down = edge < edges - 1, edge > 0

    def forward(source, d):
        up = remote(windows_ref.at[1, source], windows_ref.at[0, source], edge_sems.at[0], d,
                    edge=jnp.minimum(edge + 1, edges - 1))
        down = remote(windows_ref.at[1, source], windows_ref.at[2, source], edge_sems.at[1], d,
                      edge=jnp.maximum(edge - 1, 0))
        return up, down

    def start_forward(source, d):
        up, down = forward(source, d)
        pl.when(has_up)(up.start)
        pl.when(has_down)(down.start)

    start_forward(leaf, 0)
    for copy in cells:
        copy.wait()
    loads[4].wait()
    group = group_ref[...].reshape(edges * group_ref.shape[1], group_ref.shape[2])
    partial = lax.dot_general(group, operator_ref[...], NT, preferred_element_type=jnp.float32)
    partial_ref[...] = partial.reshape(partial_ref.shape)
    parts = []
    for d in range(1, edges):
        to = lax.rem(edge + d, edges)
        parts.append(remote(partial_ref.at[to, pl.ds(0, count)], parts_ref.at[edge], part_sems, d, edge=to))
        parts[-1].start()
    parts_ref[edge] = partial_ref[edge, pl.ds(0, count)]

    for d in range(1, leafs):
        points[d - 1].wait()
        start_forward(lax.rem(leaf + leafs - d, leafs), d)

    @pl.when(edge == 0)
    def _():
        windows_ref[0] = jnp.zeros_like(windows_ref[0])

    @pl.when(edge == edges - 1)
    def _():
        windows_ref[2] = jnp.zeros_like(windows_ref[2])

    matrices = (weight_ref, value_ref, target_ref)
    build_layer(tiles, starts, 1, windows_ref.at[1], tiles_ref, *matrices, win=win)
    near_ref[tiles:] = jnp.zeros_like(near_ref[tiles:])
    flights = [forward(lax.rem(leaf + leafs - d, leafs), d) for d in range(leafs)]
    for up, down in flights:
        pl.when(has_down)(up.wait_recv)
    build_layer(tiles, starts, 0, windows_ref.at[0], tiles_ref, *matrices, win=win)
    for up, down in flights:
        pl.when(has_up)(down.wait_recv)
        pl.when(has_up)(up.wait_send)
        pl.when(has_down)(down.wait_send)
    build_layer(tiles, starts, 2, windows_ref.at[2], tiles_ref, *matrices, win=win)

    back = [remote(ret_ref.at[d], back_ref.at[leaf], back_sems, d, leaf=lax.rem(leaf + d, leafs))
            for d in range(1, leafs)]
    loads[3].wait()
    origin = (leaf + 1) * slots // LANES
    done, sent = 0, 1
    for end in [cut for cut in CUTS if cut < tiles] + [tiles]:
        list_steps(done, end, origin, tiles, lists_ref, tiles_ref, *matrices, near_ref)
        done = end
        while sent < leafs and (sent * slots + LANES - 1) // LANES + 1 <= done:
            to = lax.rem(leaf + sent, leafs)
            first = to * slots // LANES
            for comp in range(3):
                ret_ref[sent, comp] = near_ref[pl.ds(first, win), comp, :]
            back[sent - 1].start()
            sent += 1
    first = leaf * slots // LANES
    for comp in range(3):
        back_ref[leaf, comp] = near_ref[pl.ds(first, win), comp, :]
    for copy in parts:
        copy.wait()
    share = parts_ref.shape[2]
    for e in range(edges):
        whole_ref[:, e * share : (e + 1) * share] = parts_ref[e]
    for c in range(count):
        for k in range(3):
            self_ref[k : k + 1, c * NPT : (c + 1) * NPT] = whole_ref[c : c + 1, k * NPT : (k + 1) * NPT]
    for copy in back:
        copy.wait()
    gather(leafs, lambda o, comp: back_ref[o, comp], row_ref, lane_ref, self_ref, out_ref)


VM = pl.BlockSpec(memory_space=pltpu.VMEM)
PARAMS = pltpu.CompilerParams(vmem_limit_bytes=48 * 2**20)


def self_part(density):
    cell_count = density.shape[1] // NPT
    return density.reshape(3, cell_count, NPT).transpose(1, 0, 2).reshape(cell_count, 3 * NPT)


def fast(positions, density, self_operator, owner, near_tiles):
    points = density.shape[1]
    cell_count = points // NPT
    leafs = lax.axis_size("leaf")
    slots = 3 * points // (2 * leafs)
    tiles = slots * leafs // LANES
    starts = [l * slots // LANES for l in range(leafs)]
    win = max((l * slots % LANES + slots - 1) // LANES + 1 for l in range(leafs))
    padded_tiles = -(-max(tiles, starts[-1] + win) // 8) * 8
    rows = leafs * win
    f32, bf16 = jnp.float32, jnp.bfloat16
    shape = jax.ShapeDtypeStruct

    edges = lax.axis_size("edge")
    matrices = [
        pltpu.VMEM((3, padded_tiles, 8, LANES), f32),
        pltpu.VMEM((3 * tiles, 8 * GROUPS, 2 * LANES), bf16),
        pltpu.VMEM((3 * tiles, 16, 4 * LANES), bf16),
        pltpu.VMEM((tiles, 8 * GROUPS, LANES), bf16),
        pltpu.VMEM((padded_tiles, 8, LANES), f32),
    ]
    if leafs <= 8:
        group = -(-cell_count // 16) * 16
        sent = -(-9 * win // 16) * 16
        sems = pltpu.SemaphoreType.DMA
        return pl.pallas_call(
            functools.partial(fused_kernel, leafs, edges, slots, tiles, starts),
            out_shape=shape((3, points), f32),
            in_specs=[pl.BlockSpec(memory_space=pltpu.HBM)] * 5,
            out_specs=VM,
            scratch_shapes=[
                pltpu.SMEM((3, tiles), jnp.int32),
                pltpu.VMEM((1, points), jnp.int32),
                pltpu.VMEM((3, points), f32),
                pltpu.VMEM((3, points), bf16),
                pltpu.VMEM(self_operator.shape, bf16),
                pltpu.VMEM((group, 3 * NPT), bf16),
                pltpu.VMEM((group, 3 * NPT), f32),
                pltpu.VMEM((rows, points), bf16),
                pltpu.VMEM((LANES, points), bf16),
                pltpu.VMEM((9 * rows, points), bf16),
                pltpu.VMEM((leafs, sent, LANES), bf16),
                pltpu.VMEM((3, leafs, sent, LANES), bf16),
                *matrices,
                pltpu.VMEM((leafs, 3, win, LANES), f32),
                pltpu.VMEM((leafs, 3, win, LANES), f32),
                pltpu.VMEM((edges, group, 3 * NPT), bf16),
                pltpu.VMEM((edges, group, self_operator.shape[0]), f32),
                pltpu.VMEM((edges, cell_count, self_operator.shape[0]), f32),
                pltpu.VMEM((cell_count, 3 * NPT), f32),
                pltpu.VMEM((3, points), f32),
                sems((5,)), sems((2, edges)), sems((2, edges)), sems((2, leafs)), sems((2, 2, leafs)),
                sems((2, leafs)),
            ],
            compiler_params=pltpu.CompilerParams(
                vmem_limit_bytes=62 * 2**20, collective_id=0, has_side_effects=True
            ),
            name="fused",
        )(near_tiles.T, owner.reshape(1, points), positions, density, self_operator)

    send, row_hot, lane_hot = pl.pallas_call(
        functools.partial(pre_kernel, leafs, slots),
        out_shape=(shape((leafs, 6, win, LANES), f32), shape((rows, points), bf16),
                   shape((LANES, points), bf16)),
        in_specs=[VM] * 3, out_specs=(VM,) * 3,
        scratch_shapes=[pltpu.VMEM((12 * rows, points), bf16)],
        compiler_params=PARAMS, name="pre",
    )(owner.reshape(1, points), positions, density)
    received = lax.all_to_all(send, "leaf", split_axis=0, concat_axis=0, tiled=True)
    up = [(i, i + 1) for i in range(edges - 1)]
    low = lax.ppermute(received, "edge", up)
    high = lax.ppermute(received, "edge", [(b, a) for a, b in up])

    group_rows = lax.all_gather(self_part(density), "edge", axis=0, tiled=True)
    partial_rows = lax.dot_general(group_rows, self_operator, NT, preferred_element_type=f32)
    rows_back = lax.all_to_all(partial_rows, "edge", split_axis=0, concat_axis=1, tiled=True)
    self_velocity = rows_back.reshape(cell_count, 3, NPT).transpose(1, 0, 2).reshape(3, points)

    result = pl.pallas_call(
        functools.partial(near_kernel, tiles, starts),
        out_shape=shape((leafs, 3, win, LANES), f32),
        in_specs=[pl.BlockSpec(memory_space=pltpu.SMEM), VM, VM, VM], out_specs=VM,
        scratch_shapes=matrices,
        compiler_params=PARAMS, name="near",
    )(near_tiles.T, received, low, high)
    back = lax.all_to_all(result, "leaf", split_axis=0, concat_axis=0, tiled=True)
    return pl.pallas_call(
        functools.partial(post_kernel, leafs),
        out_shape=shape((3, points), f32),
        in_specs=[VM] * 4, out_specs=VM, compiler_params=PARAMS, name="post",
    )(back, row_hot, lane_hot, self_velocity)


def solution(mesh):
    placed = (
        P(None, ("leaf", "edge")),
        P(None, ("leaf", "edge")),
        P("edge", None),
        P(("leaf", "edge"), None),
        P(("leaf", "edge"), None),
    )
    return jax.shard_map(
        fast, mesh=mesh, in_specs=placed, out_specs=P(None, ("leaf", "edge")), check_vma=False
    )
```

```python
import functools
import math

import jax
import jax.numpy as jnp
from jax import lax
from jax.experimental import pallas as pl
from jax.experimental.pallas import tpu as pltpu
from jax.sharding import PartitionSpec as P

NPT = 544
LANES = 128
GROUPS = 4
CUTS = (33, 46)

reg_square = 0.05
kernel_scale = 1.0 / (8.0 * math.pi)
NT = (((1,), (1,)), ((), ()))
TN = (((0,), (0,)), ((), ()))


def split3(x):
    hi = x.astype(jnp.bfloat16).astype(jnp.float32)
    rest = x - hi
    mid = rest.astype(jnp.bfloat16).astype(jnp.float32)
    return hi, mid, rest - mid


def split2(x):
    hi = x.astype(jnp.bfloat16)
    return hi, (x - hi.astype(jnp.float32)).astype(jnp.bfloat16)


def onehots(leafs, offset, own_ref, row_ref, lane_ref):
    points = own_ref.shape[1]
    win = row_ref.shape[0] // leafs
    chunks = points // LANES
    own = own_ref[...]
    ids = lax.broadcasted_iota(jnp.int32, (leafs, LANES), 0)
    hot = [jnp.where(own[:, c * LANES : (c + 1) * LANES] == ids, 1.0, 0.0) for c in range(chunks)]
    stacked = jnp.concatenate(hot, axis=0).astype(jnp.bfloat16)
    before = lax.broadcasted_iota(jnp.int32, (LANES, 2 * LANES), 0)
    after = lax.broadcasted_iota(jnp.int32, (LANES, 2 * LANES), 1)
    prefix = jnp.where((before < after), 1.0, 0.0).astype(jnp.bfloat16)
    counts = jnp.dot(stacked, prefix, preferred_element_type=jnp.float32)
    carry = jnp.zeros((leafs, LANES), jnp.float32) + offset.astype(jnp.float32)
    row_ids = lax.broadcasted_iota(jnp.int32, (leafs * win, LANES), 0)
    lane_ids = lax.broadcasted_iota(jnp.int32, (LANES, LANES), 0)
    for c in range(chunks):
        block = slice(c * leafs, (c + 1) * leafs)
        here = slice(c * LANES, (c + 1) * LANES)
        place = hot[c] * (counts[block, :LANES] + carry)
        carry = carry + counts[block, LANES:]
        slot = jnp.sum(place, axis=0, keepdims=True).astype(jnp.int32)
        row = own[:, here] * win + (slot >> 7)
        row_ref[:, here] = jnp.where(row == row_ids, 1.0, 0.0).astype(jnp.bfloat16)
        lane_ref[:, here] = jnp.where((slot & 127) == lane_ids, 1.0, 0.0).astype(jnp.bfloat16)


def scatter(leafs, pos_ref, den_ref, row_ref, lane_ref, spread_ref, send_ref):
    rows = row_ref.shape[0]
    win = rows // leafs
    pos = pos_ref[...]
    den = den_ref[...].astype(jnp.float32)
    parts = split3(pos)
    for k in range(12):
        part = den if k >= 9 else parts[k % 3]
        comp = k - 9 if k >= 9 else k // 3
        line = jnp.broadcast_to(part[comp : comp + 1], (16, pos.shape[1])).astype(jnp.bfloat16)
        for r in range(0, rows, 16):
            spread_ref[k * rows + r : k * rows + r + 16, :] = row_ref[r : r + 16, :] * line
    for begin, end in ((0, 6), (6, 12)):
        placed = lax.dot_general(
            spread_ref[begin * rows : end * rows, :], lane_ref[...], NT, preferred_element_type=jnp.float32
        )
        parts = [placed[r : r + rows] for r in range(0, (end - begin) * rows, rows)]
        if begin < 9:
            totals = [parts[r] + parts[r + 1] + parts[r + 2] for r in range(0, min(end, 9) - begin, 3)]
            totals += parts[9 - begin :]
        else:
            totals = parts
        for k, total in enumerate(totals):
            comp = begin // 3 + k
            for o in range(leafs):
                send_ref[o, comp] = total[o * win : (o + 1) * win]


def scatter_halves(leafs, pos_ref, den_ref, row_ref, lane_ref, spread_ref, send_ref):
    rows = row_ref.shape[0]
    win = rows // leafs
    pos = pos_ref[...]
    den = den_ref[...].astype(jnp.float32)
    high = pos.astype(jnp.bfloat16).astype(jnp.float32)
    parts = (high, pos - high)
    for k in range(9):
        part, comp = (parts[k % 2], k // 2) if k < 6 else (den, k - 6)
        line = jnp.broadcast_to(part[comp : comp + 1], (16, pos.shape[1])).astype(jnp.bfloat16)
        for r in range(0, rows, 16):
            spread_ref[k * rows + r : k * rows + r + 16, :] = row_ref[r : r + 16, :] * line
    placed = []
    for begin, end in ((0, 5), (5, 9)):
        found = lax.dot_general(
            spread_ref[begin * rows : end * rows, :], lane_ref[...], NT, preferred_element_type=jnp.float32
        )
        placed += [found[k * rows : (k + 1) * rows] for k in range(end - begin)]
    empty = jnp.zeros((send_ref.shape[1] - 9 * win, LANES), jnp.float32)
    for o in range(leafs):
        here = [part[o * win : (o + 1) * win] for part in placed] + [empty]
        send_ref[o] = jnp.concatenate(here, axis=0).astype(jnp.bfloat16)


def add_window(start, win, window, tiles_ref):
    window = window.astype(jnp.float32)
    parts = [window[k * win : (k + 1) * win] for k in range(9)]
    comps = [parts[0] + parts[1], parts[2] + parts[3], parts[4] + parts[5]] + parts[6:]
    for comp in range(6):
        tiles_ref[pl.ds(start, win), comp, :] += comps[comp]


def assemble_halves(starts, win, recv_ref, tiles_ref):
    tiles_ref[...] = jnp.zeros_like(tiles_ref)
    for l, start in enumerate(starts):
        add_window(start, win, recv_ref[l], tiles_ref)


def assemble(starts, recv_ref, tiles_ref):
    tiles_ref[...] = jnp.zeros_like(tiles_ref)
    win = recv_ref.shape[2]
    for l, start in enumerate(starts):
        for comp in range(6):
            tiles_ref[start : start + win, comp, :] += recv_ref[l, comp]


def features(tile, weight_ref, value_ref, target_ref):
    row = lax.broadcasted_iota(jnp.int32, (8, LANES), 0)
    first, last = row < 3, row == 7
    one = jnp.where(row == 6, 1.0, 0.0)
    pos = jnp.where(first, tile, 0.0)
    force = jnp.where(first, pltpu.roll(tile, 5, 0), 0.0)
    twice = force + jnp.where(first, 0.0, tile)
    hi, mid, low = split3(pos)
    hi_next, mid_next, low_next = (pltpu.roll(part, 3, 0) for part in (hi, mid, low))
    square = jnp.sum(pos * pos, axis=0, keepdims=True)
    along = jnp.sum(pos * force, axis=0, keepdims=True)
    zero = jnp.zeros_like(pos)
    pairs = (hi + hi_next, hi + mid_next, mid + low_next)
    r2_rows = [jnp.where(last, q, one - 2.0 * pair) for q, pair in zip(split3(square), pairs)]
    df_rows = [jnp.where(last, q, f) for q, f in zip(split3(-along), (twice, force, zero))]
    weight_ref[...] = jnp.concatenate(
        [jnp.concatenate(r2_rows + [zero], axis=0), jnp.concatenate(df_rows + [zero], axis=0)], axis=1
    ).astype(jnp.bfloat16)
    if target_ref is not None:
        pairs = (hi + mid_next, low + hi_next, mid + hi_next)
        fixed = jnp.where(last, 1.0, 0.0)
        rows = [fixed + pair + one * q for q, pair in zip(split3(square + reg_square), pairs)]
        target_ref[...] = jnp.concatenate(rows + [zero], axis=0).astype(jnp.bfloat16)
    a_low = one - hi
    value = jnp.concatenate([force, force, a_low - mid_next, a_low], axis=1)
    value_ref[...] = jnp.concatenate([value, jnp.zeros_like(value)], axis=0).astype(jnp.bfloat16)


def near_tile(tile, target, sources):
    blocks, values = [], []
    for weight, value in sources:
        both = lax.dot_general(weight, target, TN, preferred_element_type=jnp.float32)
        inverse = lax.rsqrt(both[:LANES])
        along = both[LANES:] * inverse * (inverse * inverse)
        blocks.extend(split2(inverse) + split2(along))
        values.append(value)
    sums = jnp.dot(
        jnp.concatenate(values, axis=1), jnp.concatenate(blocks, axis=0),
        preferred_element_type=jnp.float32,
    )[:8]
    row = lax.broadcasted_iota(jnp.int32, (8, LANES), 0)
    pos = jnp.where(row < 3, tile, 0.0)
    return (sums + pltpu.roll(sums, 5, 0) + pos * sums[6:7]) * kernel_scale


def pair_sums(target, sources):
    weights = jnp.concatenate([weight for weight, _ in sources], axis=1)
    both = lax.dot_general(target, weights, TN, preferred_element_type=jnp.float32)
    blocks = []
    for s in range(len(sources)):
        first = 2 * LANES * s
        inverse = lax.rsqrt(both[:, first : first + LANES])
        along = both[:, first + LANES : first + 2 * LANES] * inverse * (inverse * inverse)
        blocks.extend(split2(inverse) + split2(along))
    return lax.dot_general(
        jnp.concatenate([value for _, value in sources], axis=1), jnp.concatenate(blocks, axis=1), NT,
        preferred_element_type=jnp.float32,
    )[:8]


def list_steps(begin, end, origin, tiles, lists_ref, tiles_ref, weight_ref, value_ref, target_ref, near_ref):
    row = lax.broadcasted_iota(jnp.int32, (8, LANES), 0)

    def step(i, carry):
        j = lax.rem(origin + i, tiles)
        indices = [tiles + j] + [lists_ref[column, j] for column in range(3)]
        sums = pair_sums(target_ref[j], [(weight_ref[s], value_ref[s]) for s in indices])
        pos = jnp.where(row < 3, tiles_ref[1, j], 0.0)
        near_ref[j] = (sums + pltpu.roll(sums, 5, 0) + pos * sums[6:7]) * kernel_scale
        return carry

    lax.fori_loop(begin, end, step, 0, unroll=end - begin)


def gather(leafs, get_near, row_ref, lane_ref, self_ref, out_ref):
    rows = row_ref.shape[0]
    points = out_ref.shape[1]
    split = []
    for comp in range(3):
        block = jnp.concatenate([get_near(o, comp) for o in range(leafs)], axis=0)
        split.append(jnp.concatenate(split2(block), axis=1))
    near = jnp.concatenate(split, axis=0)
    for begin in range(0, points, 2 * LANES):
        here = slice(begin, begin + 2 * LANES)
        lane = lane_ref[:, here]
        found = jnp.dot(
            near, jnp.concatenate([lane, lane], axis=0), preferred_element_type=jnp.float32
        )
        row = row_ref[:, here].astype(jnp.float32)
        for comp in range(3):
            picked = found[comp * rows : (comp + 1) * rows] * row
            out_ref[comp : comp + 1, here] = (
                jnp.sum(picked, axis=0, keepdims=True) + self_ref[comp : comp + 1, here]
            )


def pre_kernel(leafs, slots, own_ref, pos_ref, den_ref, send_ref, row_ref, lane_ref, spread_ref):
    offset = lax.rem(lax.axis_index("leaf") * slots, LANES)
    onehots(leafs, offset, own_ref, row_ref, lane_ref)
    scatter(leafs, pos_ref, den_ref, row_ref, lane_ref, spread_ref, send_ref)


def build_layer(tiles, starts, layer, recv, tiles_ref, weight_ref, value_ref, target_ref, win=None):
    if win is None:
        assemble(starts, recv, tiles_ref.at[layer])
    elif layer != 1:
        assemble_halves(starts, win, recv, tiles_ref.at[layer])

    def build(j, carry):
        index = layer * tiles + j
        features(tiles_ref[layer, j], weight_ref.at[index], value_ref.at[index],
                 target_ref.at[j] if layer == 1 else None)
        return carry

    lax.fori_loop(0, tiles, build, 0, unroll=17)


def near_steps(begin, end, tiles, lists_ref, tiles_ref, weight_ref, value_ref, target_ref, near_ref, unroll):
    def step(j, carry):
        indices = [tiles + j] + [lists_ref[column, j] for column in range(3)]
        near_ref[j] = near_tile(tiles_ref[1, j], target_ref[j],
                                [(weight_ref[i], value_ref[i]) for i in indices])
        return carry

    lax.fori_loop(begin, end, step, 0, unroll=unroll)


def near_kernel(tiles, starts, lists_ref, own_ref, low_ref, high_ref, ret_ref, tiles_ref, *matrices):
    *features_refs, near_ref = matrices
    for layer, recv in enumerate((low_ref, own_ref, high_ref)):
        build_layer(tiles, starts, layer, recv, tiles_ref, *features_refs)
    near_ref[...] = jnp.zeros_like(near_ref)
    near_steps(0, tiles, tiles, lists_ref, tiles_ref, *matrices, 3)
    for l, start in enumerate(starts):
        for comp in range(3):
            ret_ref[l, comp] = near_ref[start : start + ret_ref.shape[2], comp, :]


def post_kernel(leafs, back_ref, row_ref, lane_ref, self_ref, out_ref):
    gather(leafs, lambda o, comp: back_ref[o, comp], row_ref, lane_ref, self_ref, out_ref)


def fused_kernel(leafs, edges, slots, tiles, starts, lists_hbm, own_hbm, pos_hbm, den_hbm, operator_hbm,
                 out_ref, lists_ref, own_ref, pos_ref, den_ref, operator_ref, cells_ref, wide_ref, row_ref, lane_ref, spread_ref, send_ref, windows_ref,
                 tiles_ref, weight_ref, value_ref, target_ref, near_ref, ret_ref, back_ref,
                 group_ref, partial_ref, parts_ref, whole_ref, self_ref,
                 load_sems, cell_sems, part_sems, point_sems, edge_sems, back_sems):
    loads = [pltpu.make_async_copy(own_hbm, own_ref, load_sems.at[0]),
             pltpu.make_async_copy(pos_hbm, pos_ref, load_sems.at[1]),
             pltpu.make_async_copy(den_hbm, den_ref, load_sems.at[2]),
             pltpu.make_async_copy(lists_hbm, lists_ref, load_sems.at[3]),
             pltpu.make_async_copy(operator_hbm, operator_ref, load_sems.at[4])]
    for load in loads:
        load.start()
    win = ret_ref.shape[2]
    leaf, edge = lax.axis_index("leaf"), lax.axis_index("edge")
    barrier = pltpu.get_barrier_semaphore()
    for d in range(1, leafs):
        pl.semaphore_signal(barrier, inc=1, device_id={"leaf": lax.rem(leaf + d, leafs)})
    for d in range(1, edges):
        pl.semaphore_signal(barrier, inc=1, device_id={"edge": lax.rem(edge + d, edges)})

    def remote(src, dst, sems, index, **device):
        return pltpu.make_async_remote_copy(
            src_ref=src, dst_ref=dst, send_sem=sems.at[0, index], recv_sem=sems.at[1, index],
            device_id=device,
        )

    loads[0].wait()
    onehots(leafs, lax.rem(leaf * slots, LANES), own_ref, row_ref, lane_ref)
    loads[1].wait()
    loads[2].wait()
    scatter_halves(leafs, pos_ref, den_ref, row_ref, lane_ref, spread_ref, send_ref)
    pl.semaphore_wait(barrier, leafs + edges - 2)

    points = []
    for d in range(1, leafs):
        to = lax.rem(leaf + d, leafs)
        points.append(remote(send_ref.at[to], windows_ref.at[1, leaf], point_sems, d, leaf=to))
        points[-1].start()
    count = parts_ref.shape[1]
    wide_ref[...] = jnp.zeros_like(wide_ref)
    dense = den_ref[...].astype(jnp.float32)
    for c in range(count):
        for k in range(3):
            wide_ref[c : c + 1, k * NPT : (k + 1) * NPT] = dense[k : k + 1, c * NPT : (c + 1) * NPT]
    cells_ref[...] = wide_ref[...].astype(jnp.bfloat16)
    cells = []
    for d in range(1, edges):
        to = lax.rem(edge + d, edges)
        cells.append(remote(cells_ref, group_ref.at[edge], cell_sems, d, edge=to))
        cells[-1].start()
    windows_ref[1, leaf] = send_ref[leaf]
    group_ref[edge] = cells_ref[...]

    has_up, has_down = edge < edges - 1, edge > 0

    def forward(source, d):
        up = remote(windows_ref.at[1, source], windows_ref.at[0, source], edge_sems.at[0], d,
                    edge=jnp.minimum(edge + 1, edges - 1))
        down = remote(windows_ref.at[1, source], windows_ref.at[2, source], edge_sems.at[1], d,
                      edge=jnp.maximum(edge - 1, 0))
        return up, down

    def start_forward(source, d):
        up, down = forward(source, d)
        pl.when(has_up)(up.start)
        pl.when(has_down)(down.start)

    start_forward(leaf, 0)
    tiles_ref[1] = jnp.zeros_like(tiles_ref[1])
    add_window(leaf * slots // LANES, win, send_ref[leaf], tiles_ref.at[1])
    for copy in cells:
        copy.wait()
    loads[4].wait()
    group = group_ref[...].reshape(edges * group_ref.shape[1], group_ref.shape[2])
    partial = lax.dot_general(group, operator_ref[...], NT, preferred_element_type=jnp.float32)
    partial_ref[...] = partial.reshape(partial_ref.shape)
    parts = []
    for d in range(1, edges):
        to = lax.rem(edge + d, edges)
        parts.append(remote(partial_ref.at[to, pl.ds(0, count)], parts_ref.at[edge], part_sems, d, edge=to))
        parts[-1].start()
    parts_ref[edge] = partial_ref[edge, pl.ds(0, count)]

    for d in range(1, leafs):
        points[d - 1].wait()
        source = lax.rem(leaf + leafs - d, leafs)
        start_forward(source, d)
        add_window(source * slots // LANES, win, windows_ref[1, source], tiles_ref.at[1])

    @pl.when(edge == 0)
    def _():
        windows_ref[0] = jnp.zeros_like(windows_ref[0])

    @pl.when(edge == edges - 1)
    def _():
        windows_ref[2] = jnp.zeros_like(windows_ref[2])

    matrices = (weight_ref, value_ref, target_ref)
    build_layer(tiles, starts, 1, windows_ref.at[1], tiles_ref, *matrices, win=win)
    near_ref[tiles:] = jnp.zeros_like(near_ref[tiles:])
    flights = [forward(lax.rem(leaf + leafs - d, leafs), d) for d in range(leafs)]
    for up, down in flights:
        pl.when(has_down)(up.wait_recv)
    build_layer(tiles, starts, 0, windows_ref.at[0], tiles_ref, *matrices, win=win)
    for up, down in flights:
        pl.when(has_up)(down.wait_recv)
        pl.when(has_up)(up.wait_send)
        pl.when(has_down)(down.wait_send)
    build_layer(tiles, starts, 2, windows_ref.at[2], tiles_ref, *matrices, win=win)

    back = [remote(ret_ref.at[d], back_ref.at[leaf], back_sems, d, leaf=lax.rem(leaf + d, leafs))
            for d in range(1, leafs)]
    loads[3].wait()
    origin = (leaf + 1) * slots // LANES
    done, sent = 0, 1
    for end in [cut for cut in CUTS if cut < tiles] + [tiles]:
        list_steps(done, end, origin, tiles, lists_ref, tiles_ref, *matrices, near_ref)
        done = end
        while sent < leafs and (sent * slots + LANES - 1) // LANES + 1 <= done:
            to = lax.rem(leaf + sent, leafs)
            first = to * slots // LANES
            for comp in range(3):
                ret_ref[sent, comp] = near_ref[pl.ds(first, win), comp, :]
            back[sent - 1].start()
            sent += 1
    first = leaf * slots // LANES
    for comp in range(3):
        back_ref[leaf, comp] = near_ref[pl.ds(first, win), comp, :]
    for copy in parts:
        copy.wait()
    share = parts_ref.shape[2]
    for e in range(edges):
        whole_ref[:, e * share : (e + 1) * share] = parts_ref[e]
    for c in range(count):
        for k in range(3):
            self_ref[k : k + 1, c * NPT : (c + 1) * NPT] = whole_ref[c : c + 1, k * NPT : (k + 1) * NPT]
    for copy in back:
        copy.wait()
    gather(leafs, lambda o, comp: back_ref[o, comp], row_ref, lane_ref, self_ref, out_ref)


VM = pl.BlockSpec(memory_space=pltpu.VMEM)
PARAMS = pltpu.CompilerParams(vmem_limit_bytes=48 * 2**20)


def self_part(density):
    cell_count = density.shape[1] // NPT
    return density.reshape(3, cell_count, NPT).transpose(1, 0, 2).reshape(cell_count, 3 * NPT)


def fast(positions, density, self_operator, owner, near_tiles):
    points = density.shape[1]
    cell_count = points // NPT
    leafs = lax.axis_size("leaf")
    slots = 3 * points // (2 * leafs)
    tiles = slots * leafs // LANES
    starts = [l * slots // LANES for l in range(leafs)]
    win = max((l * slots % LANES + slots - 1) // LANES + 1 for l in range(leafs))
    padded_tiles = -(-max(tiles, starts[-1] + win) // 8) * 8
    rows = leafs * win
    f32, bf16 = jnp.float32, jnp.bfloat16
    shape = jax.ShapeDtypeStruct

    edges = lax.axis_size("edge")
    matrices = [
        pltpu.VMEM((3, padded_tiles, 8, LANES), f32),
        pltpu.VMEM((3 * tiles, 8 * GROUPS, 2 * LANES), bf16),
        pltpu.VMEM((3 * tiles, 16, 4 * LANES), bf16),
        pltpu.VMEM((tiles, 8 * GROUPS, LANES), bf16),
        pltpu.VMEM((padded_tiles, 8, LANES), f32),
    ]
    if leafs <= 8:
        group = -(-cell_count // 16) * 16
        sent = -(-9 * win // 16) * 16
        sems = pltpu.SemaphoreType.DMA
        return pl.pallas_call(
            functools.partial(fused_kernel, leafs, edges, slots, tiles, starts),
            out_shape=shape((3, points), f32),
            in_specs=[pl.BlockSpec(memory_space=pltpu.HBM)] * 5,
            out_specs=VM,
            scratch_shapes=[
                pltpu.SMEM((3, tiles), jnp.int32),
                pltpu.VMEM((1, points), jnp.int32),
                pltpu.VMEM((3, points), f32),
                pltpu.VMEM((3, points), bf16),
                pltpu.VMEM(self_operator.shape, bf16),
                pltpu.VMEM((group, 3 * NPT), bf16),
                pltpu.VMEM((group, 3 * NPT), f32),
                pltpu.VMEM((rows, points), bf16),
                pltpu.VMEM((LANES, points), bf16),
                pltpu.VMEM((9 * rows, points), bf16),
                pltpu.VMEM((leafs, sent, LANES), bf16),
                pltpu.VMEM((3, leafs, sent, LANES), bf16),
                *matrices,
                pltpu.VMEM((leafs, 3, win, LANES), f32),
                pltpu.VMEM((leafs, 3, win, LANES), f32),
                pltpu.VMEM((edges, group, 3 * NPT), bf16),
                pltpu.VMEM((edges, group, self_operator.shape[0]), f32),
                pltpu.VMEM((edges, cell_count, self_operator.shape[0]), f32),
                pltpu.VMEM((cell_count, 3 * NPT), f32),
                pltpu.VMEM((3, points), f32),
                sems((5,)), sems((2, edges)), sems((2, edges)), sems((2, leafs)), sems((2, 2, leafs)),
                sems((2, leafs)),
            ],
            compiler_params=pltpu.CompilerParams(
                vmem_limit_bytes=62 * 2**20, collective_id=0, has_side_effects=True
            ),
            name="fused",
        )(near_tiles.T, owner.reshape(1, points), positions, density, self_operator)

    send, row_hot, lane_hot = pl.pallas_call(
        functools.partial(pre_kernel, leafs, slots),
        out_shape=(shape((leafs, 6, win, LANES), f32), shape((rows, points), bf16),
                   shape((LANES, points), bf16)),
        in_specs=[VM] * 3, out_specs=(VM,) * 3,
        scratch_shapes=[pltpu.VMEM((12 * rows, points), bf16)],
        compiler_params=PARAMS, name="pre",
    )(owner.reshape(1, points), positions, density)
    received = lax.all_to_all(send, "leaf", split_axis=0, concat_axis=0, tiled=True)
    up = [(i, i + 1) for i in range(edges - 1)]
    low = lax.ppermute(received, "edge", up)
    high = lax.ppermute(received, "edge", [(b, a) for a, b in up])

    group_rows = lax.all_gather(self_part(density), "edge", axis=0, tiled=True)
    partial_rows = lax.dot_general(group_rows, self_operator, NT, preferred_element_type=f32)
    rows_back = lax.all_to_all(partial_rows, "edge", split_axis=0, concat_axis=1, tiled=True)
    self_velocity = rows_back.reshape(cell_count, 3, NPT).transpose(1, 0, 2).reshape(3, points)

    result = pl.pallas_call(
        functools.partial(near_kernel, tiles, starts),
        out_shape=shape((leafs, 3, win, LANES), f32),
        in_specs=[pl.BlockSpec(memory_space=pltpu.SMEM), VM, VM, VM], out_specs=VM,
        scratch_shapes=matrices,
        compiler_params=PARAMS, name="near",
    )(near_tiles.T, received, low, high)
    back = lax.all_to_all(result, "leaf", split_axis=0, concat_axis=0, tiled=True)
    return pl.pallas_call(
        functools.partial(post_kernel, leafs),
        out_shape=shape((3, points), f32),
        in_specs=[VM] * 4, out_specs=VM, compiler_params=PARAMS, name="post",
    )(back, row_hot, lane_hot, self_velocity)


def solution(mesh):
    placed = (
        P(None, ("leaf", "edge")),
        P(None, ("leaf", "edge")),
        P("edge", None),
        P(("leaf", "edge"), None),
        P(("leaf", "edge"), None),
    )
    return jax.shard_map(
        fast, mesh=mesh, in_specs=placed, out_specs=P(None, ("leaf", "edge")), check_vma=False
    )
```

```python
import functools
import math

import jax
import jax.numpy as jnp
from jax import lax
from jax.experimental import pallas as pl
from jax.experimental.pallas import tpu as pltpu
from jax.sharding import PartitionSpec as P

NPT = 544
LANES = 128
GROUPS = 4
CUTS = (33, 46)

reg_square = 0.05
kernel_scale = 1.0 / (8.0 * math.pi)
NT = (((1,), (1,)), ((), ()))
TN = (((0,), (0,)), ((), ()))


def split3(x):
    hi = x.astype(jnp.bfloat16).astype(jnp.float32)
    rest = x - hi
    mid = rest.astype(jnp.bfloat16).astype(jnp.float32)
    return hi, mid, rest - mid


def split2(x):
    hi = x.astype(jnp.bfloat16)
    return hi, (x - hi.astype(jnp.float32)).astype(jnp.bfloat16)


def onehots(leafs, offset, own_ref, row_ref, lane_ref):
    points = own_ref.shape[1]
    win = row_ref.shape[0] // leafs
    chunks = points // LANES
    own = own_ref[...]
    ids = lax.broadcasted_iota(jnp.int32, (leafs, LANES), 0)
    hot = [jnp.where(own[:, c * LANES : (c + 1) * LANES] == ids, 1.0, 0.0) for c in range(chunks)]
    stacked = jnp.concatenate(hot, axis=0).astype(jnp.bfloat16)
    before = lax.broadcasted_iota(jnp.int32, (LANES, 2 * LANES), 0)
    after = lax.broadcasted_iota(jnp.int32, (LANES, 2 * LANES), 1)
    prefix = jnp.where((before < after), 1.0, 0.0).astype(jnp.bfloat16)
    counts = jnp.dot(stacked, prefix, preferred_element_type=jnp.float32)
    carry = jnp.zeros((leafs, LANES), jnp.float32) + offset.astype(jnp.float32)
    row_ids = lax.broadcasted_iota(jnp.int32, (leafs * win, LANES), 0)
    lane_ids = lax.broadcasted_iota(jnp.int32, (LANES, LANES), 0)
    for c in range(chunks):
        block = slice(c * leafs, (c + 1) * leafs)
        here = slice(c * LANES, (c + 1) * LANES)
        place = hot[c] * (counts[block, :LANES] + carry)
        carry = carry + counts[block, LANES:]
        slot = jnp.sum(place, axis=0, keepdims=True).astype(jnp.int32)
        row = own[:, here] * win + (slot >> 7)
        row_ref[:, here] = jnp.where(row == row_ids, 1.0, 0.0).astype(jnp.bfloat16)
        lane_ref[:, here] = jnp.where((slot & 127) == lane_ids, 1.0, 0.0).astype(jnp.bfloat16)


def scatter(leafs, pos_ref, den_ref, row_ref, lane_ref, spread_ref, send_ref):
    rows = row_ref.shape[0]
    win = rows // leafs
    pos = pos_ref[...]
    den = den_ref[...].astype(jnp.float32)
    parts = split3(pos)
    for k in range(12):
        part = den if k >= 9 else parts[k % 3]
        comp = k - 9 if k >= 9 else k // 3
        line = jnp.broadcast_to(part[comp : comp + 1], (16, pos.shape[1])).astype(jnp.bfloat16)
        for r in range(0, rows, 16):
            spread_ref[k * rows + r : k * rows + r + 16, :] = row_ref[r : r + 16, :] * line
    for begin, end in ((0, 6), (6, 12)):
        placed = lax.dot_general(
            spread_ref[begin * rows : end * rows, :], lane_ref[...], NT, preferred_element_type=jnp.float32
        )
        parts = [placed[r : r + rows] for r in range(0, (end - begin) * rows, rows)]
        if begin < 9:
            totals = [parts[r] + parts[r + 1] + parts[r + 2] for r in range(0, min(end, 9) - begin, 3)]
            totals += parts[9 - begin :]
        else:
            totals = parts
        for k, total in enumerate(totals):
            comp = begin // 3 + k
            for o in range(leafs):
                send_ref[o, comp] = total[o * win : (o + 1) * win]


def scatter_halves(leafs, pos_ref, den_ref, row_ref, lane_ref, spread_ref, send_ref):
    rows = row_ref.shape[0]
    win = rows // leafs
    pos = pos_ref[...]
    den = den_ref[...].astype(jnp.float32)
    high = pos.astype(jnp.bfloat16).astype(jnp.float32)
    parts = (high, pos - high)
    for k in range(9):
        part, comp = (parts[k % 2], k // 2) if k < 6 else (den, k - 6)
        line = jnp.broadcast_to(part[comp : comp + 1], (16, pos.shape[1])).astype(jnp.bfloat16)
        for r in range(0, rows, 16):
            spread_ref[k * rows + r : k * rows + r + 16, :] = row_ref[r : r + 16, :] * line
    placed = []
    for begin, end in ((0, 5), (5, 9)):
        found = lax.dot_general(
            spread_ref[begin * rows : end * rows, :], lane_ref[...], NT, preferred_element_type=jnp.float32
        )
        placed += [found[k * rows : (k + 1) * rows] for k in range(end - begin)]
    empty = jnp.zeros((send_ref.shape[1] - 9 * win, LANES), jnp.float32)
    for o in range(leafs):
        here = [part[o * win : (o + 1) * win] for part in placed] + [empty]
        send_ref[o] = jnp.concatenate(here, axis=0).astype(jnp.bfloat16)


def add_window(start, win, window, tiles_ref):
    window = window.astype(jnp.float32)
    parts = [window[k * win : (k + 1) * win] for k in range(9)]
    comps = [parts[0] + parts[1], parts[2] + parts[3], parts[4] + parts[5]] + parts[6:]
    for comp in range(6):
        tiles_ref[pl.ds(start, win), comp, :] += comps[comp]


def assemble_halves(starts, win, recv_ref, tiles_ref):
    tiles_ref[...] = jnp.zeros_like(tiles_ref)
    for l, start in enumerate(starts):
        add_window(start, win, recv_ref[l], tiles_ref)


def assemble(starts, recv_ref, tiles_ref):
    tiles_ref[...] = jnp.zeros_like(tiles_ref)
    win = recv_ref.shape[2]
    for l, start in enumerate(starts):
        for comp in range(6):
            tiles_ref[start : start + win, comp, :] += recv_ref[l, comp]


def features(tile, weight_ref, value_ref, target_ref):
    row = lax.broadcasted_iota(jnp.int32, (8, LANES), 0)
    first, last = row < 3, row == 7
    one = jnp.where(row == 6, 1.0, 0.0)
    pos = jnp.where(first, tile, 0.0)
    force = jnp.where(first, pltpu.roll(tile, 5, 0), 0.0)
    twice = force + jnp.where(first, 0.0, tile)
    hi, mid, low = split3(pos)
    hi_next, mid_next, low_next = (pltpu.roll(part, 3, 0) for part in (hi, mid, low))
    square = jnp.sum(pos * pos, axis=0, keepdims=True)
    along = jnp.sum(pos * force, axis=0, keepdims=True)
    zero = jnp.zeros_like(pos)
    pairs = (hi + hi_next, hi + mid_next, mid + low_next)
    r2_rows = [jnp.where(last, q, one - 2.0 * pair) for q, pair in zip(split3(square), pairs)]
    df_rows = [jnp.where(last, q, f) for q, f in zip(split3(-along), (twice, force, zero))]
    weight_ref[...] = jnp.concatenate(
        [jnp.concatenate(r2_rows + [zero], axis=0), jnp.concatenate(df_rows + [zero], axis=0)], axis=1
    ).astype(jnp.bfloat16)
    if target_ref is not None:
        pairs = (hi + mid_next, low + hi_next, mid + hi_next)
        fixed = jnp.where(last, 1.0, 0.0)
        rows = [fixed + pair + one * q for q, pair in zip(split3(square + reg_square), pairs)]
        target_ref[...] = jnp.concatenate(rows + [zero], axis=0).astype(jnp.bfloat16)
    a_low = one - hi
    value = jnp.concatenate([force, force, a_low - mid_next, a_low], axis=1)
    value_ref[...] = jnp.concatenate([value, jnp.zeros_like(value)], axis=0).astype(jnp.bfloat16)


def near_tile(tile, target, sources):
    blocks, values = [], []
    for weight, value in sources:
        both = lax.dot_general(weight, target, TN, preferred_element_type=jnp.float32)
        inverse = lax.rsqrt(both[:LANES])
        along = both[LANES:] * inverse * (inverse * inverse)
        blocks.extend(split2(inverse) + split2(along))
        values.append(value)
    sums = jnp.dot(
        jnp.concatenate(values, axis=1), jnp.concatenate(blocks, axis=0),
        preferred_element_type=jnp.float32,
    )[:8]
    row = lax.broadcasted_iota(jnp.int32, (8, LANES), 0)
    pos = jnp.where(row < 3, tile, 0.0)
    return (sums + pltpu.roll(sums, 5, 0) + pos * sums[6:7]) * kernel_scale


def pair_sums(target, sources):
    halves = []
    for s in range(0, len(sources), 2):
        weights = jnp.concatenate([weight for weight, _ in sources[s : s + 2]], axis=1)
        halves.append(lax.dot_general(target, weights, TN, preferred_element_type=jnp.float32))
    both = jnp.concatenate(halves, axis=1)
    blocks = []
    for s in range(len(sources)):
        first = 2 * LANES * s
        inverse = lax.rsqrt(both[:, first : first + LANES])
        along = both[:, first + LANES : first + 2 * LANES] * inverse * (inverse * inverse)
        blocks.extend(split2(inverse) + split2(along))
    return lax.dot_general(
        jnp.concatenate([value for _, value in sources], axis=1), jnp.concatenate(blocks, axis=1), NT,
        preferred_element_type=jnp.float32,
    )[:8]


def list_steps(begin, end, origin, tiles, lists_ref, tiles_ref, weight_ref, value_ref, target_ref, near_ref):
    row = lax.broadcasted_iota(jnp.int32, (8, LANES), 0)

    def step(i, carry):
        j = lax.rem(origin + i, tiles)
        indices = [tiles + j] + [lists_ref[column, j] for column in range(3)]
        sums = pair_sums(target_ref[j], [(weight_ref[s], value_ref[s]) for s in indices])
        pos = jnp.where(row < 3, tiles_ref[1, j], 0.0)
        near_ref[j] = (sums + pltpu.roll(sums, 5, 0) + pos * sums[6:7]) * kernel_scale
        return carry

    lax.fori_loop(begin, end, step, 0, unroll=end - begin)


def gather(leafs, get_near, row_ref, lane_ref, self_ref, out_ref):
    rows = row_ref.shape[0]
    points = out_ref.shape[1]
    split = []
    for comp in range(3):
        block = jnp.concatenate([get_near(o, comp) for o in range(leafs)], axis=0)
        split.append(jnp.concatenate(split2(block), axis=1))
    near = jnp.concatenate(split, axis=0)
    for begin in range(0, points, 2 * LANES):
        here = slice(begin, begin + 2 * LANES)
        lane = lane_ref[:, here]
        found = jnp.dot(
            near, jnp.concatenate([lane, lane], axis=0), preferred_element_type=jnp.float32
        )
        row = row_ref[:, here].astype(jnp.float32)
        for comp in range(3):
            picked = found[comp * rows : (comp + 1) * rows] * row
            out_ref[comp : comp + 1, here] = (
                jnp.sum(picked, axis=0, keepdims=True) + self_ref[comp : comp + 1, here]
            )


def pre_kernel(leafs, slots, own_ref, pos_ref, den_ref, send_ref, row_ref, lane_ref, spread_ref):
    offset = lax.rem(lax.axis_index("leaf") * slots, LANES)
    onehots(leafs, offset, own_ref, row_ref, lane_ref)
    scatter(leafs, pos_ref, den_ref, row_ref, lane_ref, spread_ref, send_ref)


def build_layer(tiles, starts, layer, recv, tiles_ref, weight_ref, value_ref, target_ref, win=None):
    if win is None:
        assemble(starts, recv, tiles_ref.at[layer])
    elif layer != 1:
        assemble_halves(starts, win, recv, tiles_ref.at[layer])

    def build(j, carry):
        index = layer * tiles + j
        features(tiles_ref[layer, j], weight_ref.at[index], value_ref.at[index],
                 target_ref.at[j] if layer == 1 else None)
        return carry

    lax.fori_loop(0, tiles, build, 0, unroll=17)


def near_steps(begin, end, tiles, lists_ref, tiles_ref, weight_ref, value_ref, target_ref, near_ref, unroll):
    def step(j, carry):
        indices = [tiles + j] + [lists_ref[column, j] for column in range(3)]
        near_ref[j] = near_tile(tiles_ref[1, j], target_ref[j],
                                [(weight_ref[i], value_ref[i]) for i in indices])
        return carry

    lax.fori_loop(begin, end, step, 0, unroll=unroll)


def near_kernel(tiles, starts, lists_ref, own_ref, low_ref, high_ref, ret_ref, tiles_ref, *matrices):
    *features_refs, near_ref = matrices
    for layer, recv in enumerate((low_ref, own_ref, high_ref)):
        build_layer(tiles, starts, layer, recv, tiles_ref, *features_refs)
    near_ref[...] = jnp.zeros_like(near_ref)
    near_steps(0, tiles, tiles, lists_ref, tiles_ref, *matrices, 3)
    for l, start in enumerate(starts):
        for comp in range(3):
            ret_ref[l, comp] = near_ref[start : start + ret_ref.shape[2], comp, :]


def post_kernel(leafs, back_ref, row_ref, lane_ref, self_ref, out_ref):
    gather(leafs, lambda o, comp: back_ref[o, comp], row_ref, lane_ref, self_ref, out_ref)


def fused_kernel(leafs, edges, slots, tiles, starts, lists_hbm, own_hbm, pos_hbm, den_hbm, operator_hbm,
                 out_ref, lists_ref, own_ref, pos_ref, den_ref, operator_ref, cells_ref, wide_ref, row_ref, lane_ref, spread_ref, send_ref, windows_ref,
                 tiles_ref, weight_ref, value_ref, target_ref, near_ref, ret_ref, back_ref,
                 group_ref, partial_ref, parts_ref, whole_ref, self_ref,
                 load_sems, cell_sems, part_sems, point_sems, edge_sems, back_sems):
    loads = [pltpu.make_async_copy(own_hbm, own_ref, load_sems.at[0]),
             pltpu.make_async_copy(pos_hbm, pos_ref, load_sems.at[1]),
             pltpu.make_async_copy(den_hbm, den_ref, load_sems.at[2]),
             pltpu.make_async_copy(lists_hbm, lists_ref, load_sems.at[3]),
             pltpu.make_async_copy(operator_hbm, operator_ref, load_sems.at[4])]
    for load in loads:
        load.start()
    win = ret_ref.shape[2]
    leaf, edge = lax.axis_index("leaf"), lax.axis_index("edge")
    barrier = pltpu.get_barrier_semaphore()
    for d in range(1, leafs):
        pl.semaphore_signal(barrier, inc=1, device_id={"leaf": lax.rem(leaf + d, leafs)})
    for d in range(1, edges):
        pl.semaphore_signal(barrier, inc=1, device_id={"edge": lax.rem(edge + d, edges)})

    def remote(src, dst, sems, index, **device):
        return pltpu.make_async_remote_copy(
            src_ref=src, dst_ref=dst, send_sem=sems.at[0, index], recv_sem=sems.at[1, index],
            device_id=device,
        )

    loads[0].wait()
    onehots(leafs, lax.rem(leaf * slots, LANES), own_ref, row_ref, lane_ref)
    loads[1].wait()
    loads[2].wait()
    scatter_halves(leafs, pos_ref, den_ref, row_ref, lane_ref, spread_ref, send_ref)
    pl.semaphore_wait(barrier, leafs + edges - 2)

    points = []
    for d in range(1, leafs):
        to = lax.rem(leaf + d, leafs)
        points.append(remote(send_ref.at[to], windows_ref.at[1, leaf], point_sems, d, leaf=to))
        points[-1].start()
    count = parts_ref.shape[1]
    wide_ref[...] = jnp.zeros_like(wide_ref)
    dense = den_ref[...].astype(jnp.float32)
    for c in range(count):
        for k in range(3):
            wide_ref[c : c + 1, k * NPT : (k + 1) * NPT] = dense[k : k + 1, c * NPT : (c + 1) * NPT]
    cells_ref[...] = wide_ref[...].astype(jnp.bfloat16)
    cells = []
    for d in range(1, edges):
        to = lax.rem(edge + d, edges)
        cells.append(remote(cells_ref, group_ref.at[edge], cell_sems, d, edge=to))
        cells[-1].start()
    windows_ref[1, leaf] = send_ref[leaf]
    group_ref[edge] = cells_ref[...]

    has_up, has_down = edge < edges - 1, edge > 0

    def forward(source, d):
        up = remote(windows_ref.at[1, source], windows_ref.at[0, source], edge_sems.at[0], d,
                    edge=jnp.minimum(edge + 1, edges - 1))
        down = remote(windows_ref.at[1, source], windows_ref.at[2, source], edge_sems.at[1], d,
                      edge=jnp.maximum(edge - 1, 0))
        return up, down

    def start_forward(source, d):
        up, down = forward(source, d)
        pl.when(has_up)(up.start)
        pl.when(has_down)(down.start)

    start_forward(leaf, 0)
    tiles_ref[1] = jnp.zeros_like(tiles_ref[1])
    add_window(leaf * slots // LANES, win, send_ref[leaf], tiles_ref.at[1])
    for copy in cells:
        copy.wait()
    loads[4].wait()
    group = group_ref[...].reshape(edges * group_ref.shape[1], group_ref.shape[2])
    partial = lax.dot_general(group, operator_ref[...], NT, preferred_element_type=jnp.float32)
    partial_ref[...] = partial.reshape(partial_ref.shape)
    parts = []
    for d in range(1, edges):
        to = lax.rem(edge + d, edges)
        parts.append(remote(partial_ref.at[to, pl.ds(0, count)], parts_ref.at[edge], part_sems, d, edge=to))
        parts[-1].start()
    parts_ref[edge] = partial_ref[edge, pl.ds(0, count)]

    for d in range(1, leafs):
        points[d - 1].wait()
        source = lax.rem(leaf + leafs - d, leafs)
        start_forward(source, d)
        add_window(source * slots // LANES, win, windows_ref[1, source], tiles_ref.at[1])

    @pl.when(edge == 0)
    def _():
        windows_ref[0] = jnp.zeros_like(windows_ref[0])

    @pl.when(edge == edges - 1)
    def _():
        windows_ref[2] = jnp.zeros_like(windows_ref[2])

    matrices = (weight_ref, value_ref, target_ref)
    build_layer(tiles, starts, 1, windows_ref.at[1], tiles_ref, *matrices, win=win)
    near_ref[tiles:] = jnp.zeros_like(near_ref[tiles:])
    flights = [forward(lax.rem(leaf + leafs - d, leafs), d) for d in range(leafs)]
    for up, down in flights:
        pl.when(has_down)(up.wait_recv)
    build_layer(tiles, starts, 0, windows_ref.at[0], tiles_ref, *matrices, win=win)
    for up, down in flights:
        pl.when(has_up)(down.wait_recv)
        pl.when(has_up)(up.wait_send)
        pl.when(has_down)(down.wait_send)
    build_layer(tiles, starts, 2, windows_ref.at[2], tiles_ref, *matrices, win=win)

    back = [remote(ret_ref.at[d], back_ref.at[leaf], back_sems, d, leaf=lax.rem(leaf + d, leafs))
            for d in range(1, leafs)]
    loads[3].wait()
    origin = (leaf + 1) * slots // LANES
    done, sent = 0, 1
    for end in [cut for cut in CUTS if cut < tiles] + [tiles]:
        list_steps(done, end, origin, tiles, lists_ref, tiles_ref, *matrices, near_ref)
        done = end
        while sent < leafs and (sent * slots + LANES - 1) // LANES + 1 <= done:
            to = lax.rem(leaf + sent, leafs)
            first = to * slots // LANES
            for comp in range(3):
                ret_ref[sent, comp] = near_ref[pl.ds(first, win), comp, :]
            back[sent - 1].start()
            sent += 1
    first = leaf * slots // LANES
    for comp in range(3):
        back_ref[leaf, comp] = near_ref[pl.ds(first, win), comp, :]
    for copy in parts:
        copy.wait()
    share = parts_ref.shape[2]
    for e in range(edges):
        whole_ref[:, e * share : (e + 1) * share] = parts_ref[e]
    for c in range(count):
        for k in range(3):
            self_ref[k : k + 1, c * NPT : (c + 1) * NPT] = whole_ref[c : c + 1, k * NPT : (k + 1) * NPT]
    for copy in back:
        copy.wait()
    gather(leafs, lambda o, comp: back_ref[o, comp], row_ref, lane_ref, self_ref, out_ref)


VM = pl.BlockSpec(memory_space=pltpu.VMEM)
PARAMS = pltpu.CompilerParams(vmem_limit_bytes=48 * 2**20)


def self_part(density):
    cell_count = density.shape[1] // NPT
    return density.reshape(3, cell_count, NPT).transpose(1, 0, 2).reshape(cell_count, 3 * NPT)


def fast(positions, density, self_operator, owner, near_tiles):
    points = density.shape[1]
    cell_count = points // NPT
    leafs = lax.axis_size("leaf")
    slots = 3 * points // (2 * leafs)
    tiles = slots * leafs // LANES
    starts = [l * slots // LANES for l in range(leafs)]
    win = max((l * slots % LANES + slots - 1) // LANES + 1 for l in range(leafs))
    padded_tiles = -(-max(tiles, starts[-1] + win) // 8) * 8
    rows = leafs * win
    f32, bf16 = jnp.float32, jnp.bfloat16
    shape = jax.ShapeDtypeStruct

    edges = lax.axis_size("edge")
    matrices = [
        pltpu.VMEM((3, padded_tiles, 8, LANES), f32),
        pltpu.VMEM((3 * tiles, 8 * GROUPS, 2 * LANES), bf16),
        pltpu.VMEM((3 * tiles, 16, 4 * LANES), bf16),
        pltpu.VMEM((tiles, 8 * GROUPS, LANES), bf16),
        pltpu.VMEM((padded_tiles, 8, LANES), f32),
    ]
    if leafs <= 8:
        group = -(-cell_count // 16) * 16
        sent = -(-9 * win // 16) * 16
        sems = pltpu.SemaphoreType.DMA
        return pl.pallas_call(
            functools.partial(fused_kernel, leafs, edges, slots, tiles, starts),
            out_shape=shape((3, points), f32),
            in_specs=[pl.BlockSpec(memory_space=pltpu.HBM)] * 5,
            out_specs=VM,
            scratch_shapes=[
                pltpu.SMEM((3, tiles), jnp.int32),
                pltpu.VMEM((1, points), jnp.int32),
                pltpu.VMEM((3, points), f32),
                pltpu.VMEM((3, points), bf16),
                pltpu.VMEM(self_operator.shape, bf16),
                pltpu.VMEM((group, 3 * NPT), bf16),
                pltpu.VMEM((group, 3 * NPT), f32),
                pltpu.VMEM((rows, points), bf16),
                pltpu.VMEM((LANES, points), bf16),
                pltpu.VMEM((9 * rows, points), bf16),
                pltpu.VMEM((leafs, sent, LANES), bf16),
                pltpu.VMEM((3, leafs, sent, LANES), bf16),
                *matrices,
                pltpu.VMEM((leafs, 3, win, LANES), f32),
                pltpu.VMEM((leafs, 3, win, LANES), f32),
                pltpu.VMEM((edges, group, 3 * NPT), bf16),
                pltpu.VMEM((edges, group, self_operator.shape[0]), f32),
                pltpu.VMEM((edges, cell_count, self_operator.shape[0]), f32),
                pltpu.VMEM((cell_count, 3 * NPT), f32),
                pltpu.VMEM((3, points), f32),
                sems((5,)), sems((2, edges)), sems((2, edges)), sems((2, leafs)), sems((2, 2, leafs)),
                sems((2, leafs)),
            ],
            compiler_params=pltpu.CompilerParams(
                vmem_limit_bytes=62 * 2**20, collective_id=0, has_side_effects=True
            ),
            name="fused",
        )(near_tiles.T, owner.reshape(1, points), positions, density, self_operator)

    send, row_hot, lane_hot = pl.pallas_call(
        functools.partial(pre_kernel, leafs, slots),
        out_shape=(shape((leafs, 6, win, LANES), f32), shape((rows, points), bf16),
                   shape((LANES, points), bf16)),
        in_specs=[VM] * 3, out_specs=(VM,) * 3,
        scratch_shapes=[pltpu.VMEM((12 * rows, points), bf16)],
        compiler_params=PARAMS, name="pre",
    )(owner.reshape(1, points), positions, density)
    received = lax.all_to_all(send, "leaf", split_axis=0, concat_axis=0, tiled=True)
    up = [(i, i + 1) for i in range(edges - 1)]
    low = lax.ppermute(received, "edge", up)
    high = lax.ppermute(received, "edge", [(b, a) for a, b in up])

    group_rows = lax.all_gather(self_part(density), "edge", axis=0, tiled=True)
    partial_rows = lax.dot_general(group_rows, self_operator, NT, preferred_element_type=f32)
    rows_back = lax.all_to_all(partial_rows, "edge", split_axis=0, concat_axis=1, tiled=True)
    self_velocity = rows_back.reshape(cell_count, 3, NPT).transpose(1, 0, 2).reshape(3, points)

    result = pl.pallas_call(
        functools.partial(near_kernel, tiles, starts),
        out_shape=shape((leafs, 3, win, LANES), f32),
        in_specs=[pl.BlockSpec(memory_space=pltpu.SMEM), VM, VM, VM], out_specs=VM,
        scratch_shapes=matrices,
        compiler_params=PARAMS, name="near",
    )(near_tiles.T, received, low, high)
    back = lax.all_to_all(result, "leaf", split_axis=0, concat_axis=0, tiled=True)
    return pl.pallas_call(
        functools.partial(post_kernel, leafs),
        out_shape=shape((3, points), f32),
        in_specs=[VM] * 4, out_specs=VM, compiler_params=PARAMS, name="post",
    )(back, row_hot, lane_hot, self_velocity)


def solution(mesh):
    placed = (
        P(None, ("leaf", "edge")),
        P(None, ("leaf", "edge")),
        P("edge", None),
        P(("leaf", "edge"), None),
        P(("leaf", "edge"), None),
    )
    return jax.shard_map(
        fast, mesh=mesh, in_specs=placed, out_specs=P(None, ("leaf", "edge")), check_vma=False
    )
```
